256 devices in a mesh: dom: 256 (over z, y, x, core).
Axes of the slice: x: 4, y: 4, z: 8, core: 2. Of those that a mesh axis runs over, the one named last changes fastest.
Arguments:
- adj_disp: float32 [1024, 33, 512], P('dom'), may hold values from -6 to 6
- adj_vel: float32 [1024, 33, 512], P('dom'), may hold values from -6 to 6
- fwd_disp: float32 [2, 1024, 33, 512], P(None, 'dom'), may hold values from -6 to 6
- shear_mod: float32 [2048, 25, 512], P('dom'), may hold values from 0.5 to 2
- inv_radius: float32 [2048, 25], P('dom'), may hold values from 0.001953125 to 0.0078125
- inv_mass: float32 [1024, 33], P('dom'), may hold values from 0.5 to 2
- mode_counts: int32 [2048], P('dom'), may hold values from 16 to 256, as said below
- rec_elem: int32 [256], P('dom'), may hold values from 0 to 2047
- rec_force: float32 [256, 2, 512], P('dom'), may hold values from -6 to 6
Outputs:
- new_disp: float32 [1024, 33, 512], P('dom')
- new_vel: float32 [1024, 33, 512], P('dom')
- kernel: float32 [2048, 25, 512], P('dom')
The draws below stay inside these ranges and needn't reach their ends.
Inputs may be any that keep to these rules, and one draw needn't show every extreme that they name: `mode_counts`: in each device's aligned block of 8 elements exactly 2 elements have more than 128 modes; in each block at least one element has 256 modes and at least one has exactly 128.
All inputs are finite; a program needn't handle non-finite values.
Results may differ from the reference program's by a relative error of at most 0.0003.
Values sent between devices are 32-bit elements; how exact they have to be, the bound alone decides.
A program may use at most 128 MiB of HBM per device.

```python
import math
import jax
import jax.numpy as jnp
import numpy as np
from jax import lax

MMAX = 256
NPHI = 512
MLOW = 128
STEPS = 2
EW = 8
EH = 1
NEH = 256
ELEMS = 2048
ROWS = 1024
NC = 33
NREC = 256


def draw_mode_counts(key, part):
    key = jax.random.fold_in(key, 11)
    per_dev = EH * EW
    blocks = ELEMS // per_dev
    high_count = per_dev // 3
    key_order, key_low, key_high = jax.random.split(key, 3)
    scores = jax.random.randint(key_order, (blocks, per_dev), 0, 1 << 20) * per_dev + jnp.arange(per_dev, dtype=jnp.int32)[None, :]
    ranking = jnp.argsort(jnp.argsort(scores, axis=1), axis=1)
    low_draw = jax.random.randint(key_low, (blocks, per_dev), MLOW // 8, MLOW + 1)
    high_draw = jax.random.randint(key_high, (blocks, per_dev), MLOW + 1, MMAX + 1)
    counts = jnp.where(ranking < high_count, high_draw, low_draw)
    counts = jnp.where(ranking == 0, MMAX, counts)
    counts = jnp.where(ranking == high_count, MLOW, counts)
    return counts.reshape(ELEMS).astype(jnp.int32)


def with_ends(values, stream_key, low, high):
    longest = values.shape.index(max(values.shape))
    spots = []
    for shift in (0, 1):
        where = [jax.random.randint(jax.random.fold_in(stream_key, axis), (), 0, length) for axis, length in enumerate(values.shape)]
        where[longest] = (where[longest] + shift) % values.shape[longest]
        spots.append(tuple(where))
    return values.at[spots[0]].set(low).at[spots[1]].set(high)


def steps_of(rng, dims, cuts, smallest, high):
    factor_of = 1.0
    for dim, parts in cuts:
        steps = jax.random.uniform(jax.random.fold_in(jax.random.fold_in(rng, 6), dim), (parts,), jnp.float32, smallest / len(cuts), high / len(cuts))
        factor_of = factor_of * jnp.repeat(jnp.exp(steps), dims[dim] // parts).reshape((-1,) + (1,) * (len(dims) - 1 - dim))
    return factor_of


def gaussian(rng, dims, spread, bound, cuts=(), kind=jnp.bfloat16):
    drawn = spread * jax.random.normal(rng, dims, jnp.float32)
    if cuts:
        drawn = drawn * steps_of(rng, dims, cuts, -0.22, 0.18)
    return jnp.clip(drawn, -bound, bound).astype(kind)


def setup_inputs(seed: int = 0) -> dict:
    key_of = jax.random.split(jax.random.key(seed), 10)
    return {
        "adj_disp": gaussian(key_of[0], (ROWS, NC, 2 * MMAX), 1.0, 6.0, ((0, 256),), jnp.float32),
        "adj_vel": gaussian(key_of[1], (ROWS, NC, 2 * MMAX), 1.0, 6.0, ((0, 256),), jnp.float32),
        "fwd_disp": gaussian(key_of[2], (STEPS, ROWS, NC, 2 * MMAX), 1.0, 6.0, ((1, 256),), jnp.float32),
        "shear_mod": jnp.clip(jnp.exp(math.log(2.0) - 1.3862944 * jax.random.uniform(key_of[3], (ELEMS, 25, NPHI), jnp.float32) ** steps_of(key_of[3], (ELEMS, 25, NPHI), ((0, 256),), -0.2, 0.2)), 0.5, 2.0),
        "inv_radius": jnp.clip(jnp.exp(math.log(0.0078125) - 1.3862944 * jax.random.uniform(key_of[4], (ELEMS, 25), jnp.float32) ** steps_of(key_of[4], (ELEMS, 25), ((0, 256),), -0.2, 0.2)), 0.001953125, 0.0078125),
        "inv_mass": jnp.clip(jnp.exp(math.log(2.0) - 1.3862944 * jax.random.uniform(key_of[5], (ROWS, NC), jnp.float32) ** steps_of(key_of[5], (ROWS, NC), ((0, 256),), -0.2, 0.2)), 0.5, 2.0),
        "mode_counts": draw_mode_counts(jax.random.fold_in(key_of[9], 71), 0),
        "rec_elem": with_ends(jax.random.randint(key_of[7], (NREC,), 0, ELEMS), jax.random.fold_in(key_of[7], 1), 0, ELEMS - 1).astype(jnp.int32),
        "rec_force": gaussian(key_of[8], (NREC, STEPS, 2 * MMAX), 1.0, 6.0, ((0, 256),), jnp.float32),
    }


GSCALE = 0.25
DTIME = 0.25

def gll_derivative():
    points = np.array([-1.0, -np.sqrt(3.0 / 7.0), 0.0, np.sqrt(3.0 / 7.0), 1.0])
    legendre = (35.0 * points ** 4 - 30.0 * points ** 2 + 3.0) / 8.0
    matrix = np.zeros((5, 5))
    for row_off in range(5):
        for col_off in range(5):
            if row_off != col_off:
                matrix[row_off, col_off] = legendre[row_off] / (legendre[col_off] * (points[row_off] - points[col_off]))
    matrix[0, 0] = -5.0
    matrix[4, 4] = 5.0
    return jnp.asarray(matrix, dtype=jnp.float32)

def dft_table(mode_width, samples):
    mode_index = jnp.arange(mode_width, dtype=jnp.int32)[:, None]
    sample_index = jnp.arange(samples, dtype=jnp.int32)[None, :]
    reduced = mode_index * sample_index % samples
    angles = 2.0 * np.pi / samples * reduced.astype(jnp.float32)
    factor = 1.0 / np.sqrt(mode_width)
    return jnp.concatenate([jnp.cos(angles) * factor, -jnp.sin(angles) * factor], axis=0)

def gather_elements(extended, elem_rows, elem_cols):
    pieces = []
    for row_off in range(5):
        for col_off in range(5):
            pieces.append(extended[row_off:row_off + 4 * elem_rows:4, col_off:col_off + 4 * elem_cols:4])
    stacked = jnp.stack(pieces, axis=2)
    return stacked.reshape(elem_rows * elem_cols, 25, extended.shape[2])

def scatter_elements(contrib, elem_rows, elem_cols, node_cols):
    channels = contrib.shape[2]
    shaped = contrib.reshape(elem_rows, elem_cols, 25, channels)
    result = jnp.zeros((4 * elem_rows + 1, node_cols, channels), jnp.float32)
    for row_off in range(5):
        for col_off in range(5):
            result = result.at[row_off:row_off + 4 * elem_rows:4, col_off:col_off + 4 * elem_cols:4].add(shaped[:, :, 5 * row_off + col_off])
    return result

def element_terms(values, fvalues, shear, inv_rad, counts, transform, mode_width):
    count_el = values.shape[0]
    samples = transform.shape[1]
    mode_index = jnp.arange(mode_width, dtype=jnp.int32)
    live_modes = (mode_index[None, :] < counts[:, None]).astype(jnp.float32)
    mode_mask = jnp.concatenate([live_modes, live_modes], axis=1)[:, None, :]
    factor = mode_index.astype(jnp.float32)
    derivative = gll_derivative()
    highest = lax.Precision.HIGHEST

    def gradients(field):
        masked = field * mode_mask
        element_grid = masked.reshape(count_el, 5, 5, 2 * mode_width)
        radial_grad = GSCALE * jnp.einsum('ik,nkjc->nijc', derivative, element_grid, precision=highest)
        lateral_grad = GSCALE * jnp.einsum('jk,nikc->nijc', derivative, element_grid, precision=highest)
        azimuth_grad = jnp.concatenate([-factor * masked[..., mode_width:], factor * masked[..., :mode_width]], axis=-1) * inv_rad[..., None]
        outputs = []
        for gradient in (radial_grad, lateral_grad, azimuth_grad):
            outputs.append(jnp.dot(gradient.reshape(count_el * 25, 2 * mode_width), transform, precision=highest))
        return outputs
    adjoint = gradients(values)
    forward = gradients(fvalues)
    flat_shear = shear.reshape(count_el * 25, samples)
    returned = []
    for physical in adjoint:
        returned.append(jnp.dot(flat_shear * physical, transform.T, precision=highest))
    radial_back = GSCALE * jnp.einsum('ik,nijc->nkjc', derivative, returned[0].reshape(count_el, 5, 5, 2 * mode_width), precision=highest)
    lateral_back = GSCALE * jnp.einsum('jk,nijc->nikc', derivative, returned[1].reshape(count_el, 5, 5, 2 * mode_width), precision=highest)
    azimuth_back = returned[2].reshape(count_el, 25, 2 * mode_width) * inv_rad[..., None]
    azimuth_back = jnp.concatenate([factor * azimuth_back[..., mode_width:], -factor * azimuth_back[..., :mode_width]], axis=-1)
    contrib = (radial_back.reshape(count_el, 25, 2 * mode_width) + lateral_back.reshape(count_el, 25, 2 * mode_width) + azimuth_back) * mode_mask
    sensitivity = forward[0] * adjoint[0] + forward[1] * adjoint[1] + forward[2] * adjoint[2]
    return (contrib, sensitivity.reshape(count_el, 25, samples))

def reference(adj_disp, adj_vel, fwd_disp, shear_mod, inv_radius, inv_mass, mode_counts, rec_elem, rec_force):
    channels = 2 * MMAX
    transform = dft_table(MMAX, NPHI)
    center_row = rec_elem // EW * 4 + 2
    center_col = rec_elem % EW * 4 + 2
    source_load = jnp.zeros((STEPS, ROWS, NC, channels), jnp.float32).at[:, center_row, center_col].add(jnp.transpose(rec_force, (1, 0, 2)))
    zero_row = jnp.zeros((1, NC, channels), jnp.float32)
    kernel = None
    for step in range(STEPS):
        extended = jnp.concatenate([adj_disp, zero_row], axis=0)
        fextended = jnp.concatenate([fwd_disp[step], zero_row], axis=0)

        def one_row(elem_row):
            row_block = lax.dynamic_slice_in_dim(extended, elem_row * 4, 5, 0)
            frow_block = lax.dynamic_slice_in_dim(fextended, elem_row * 4, 5, 0)
            first_elem = elem_row * EW
            shear = lax.dynamic_slice_in_dim(shear_mod, first_elem, EW, 0)
            inv_rad = lax.dynamic_slice_in_dim(inv_radius, first_elem, EW, 0)
            counts = lax.dynamic_slice_in_dim(mode_counts, first_elem, EW, 0)
            return element_terms(gather_elements(row_block, 1, EW), gather_elements(frow_block, 1, EW), shear, inv_rad, counts, transform, MMAX)
        contrib, sensitivity = lax.map(one_row, jnp.arange(NEH, dtype=jnp.int32))
        stiffness = scatter_elements(contrib.reshape(NEH * EW, 25, channels), NEH, EW, NC)[:ROWS]
        adj_vel = adj_vel + DTIME * inv_mass[:, :, None] * (source_load[step] - stiffness)
        adj_disp = adj_disp + DTIME * adj_vel
        sensitivity = sensitivity.reshape(ELEMS, 25, NPHI)
        kernel = sensitivity if kernel is None else kernel + sensitivity
    return (adj_disp, adj_vel, kernel)
```

```python
import functools

import jax
import jax.numpy as jnp
import ml_dtypes
import numpy as np
from jax import lax
from jax.experimental import pallas as pl
from jax.experimental.pallas import tpu as pltpu
from jax.sharding import PartitionSpec as P

GSCALE = 0.25
DTIME = 0.25
NZ, NY, NX, NCORE = 8, 4, 4, 2
NDEV = NZ * NY * NX * NCORE
BLOCKS = NCORE * NY * NX
LANES = 128
CHUNKS = 4
MODES = 256
WIDTH = 512
MESH = pl.DeviceIdType.MESH
F32 = jnp.float32
BF16 = jnp.bfloat16


def gll_derivative():
    points = np.array([-1.0, -np.sqrt(3.0 / 7.0), 0.0, np.sqrt(3.0 / 7.0), 1.0])
    legendre = (35.0 * points**4 - 30.0 * points**2 + 3.0) / 8.0
    matrix = np.zeros((5, 5))
    for row in range(5):
        for col in range(5):
            if row != col:
                matrix[row, col] = legendre[row] / (legendre[col] * (points[row] - points[col]))
    matrix[0, 0] = -5.0
    matrix[4, 4] = 5.0
    return matrix


DQ = GSCALE * gll_derivative()
DQT = DQ.T


def tables():
    mode = np.arange(MODES)[:, None]
    angle = 2.0 * np.pi * (mode * np.arange(WIDTH)[None, :] % WIDTH) / WIDTH
    scale = 1.0 / np.sqrt(MODES)
    cos, sin = np.cos(angle) * scale, np.sin(angle) * scale
    plain = np.concatenate([cos, -sin], axis=0)
    deriv = np.concatenate([-mode * sin, -mode * cos], axis=0)

    def parts(table):
        high = table.astype(ml_dtypes.bfloat16)
        low = (table - high.astype(np.float64)).astype(ml_dtypes.bfloat16)
        return high, low

    ph, plo = parts(plain)
    dh, dlo = parts(deriv)
    return np.stack([ph, dh, plo, dlo, ph.T, dh.T, plo.T, dlo.T])


def apply5(mat, x):
    even = [x[0] + x[4], x[1] + x[3]]
    odd = [x[0] - x[4], x[1] - x[3]]

    def combine(terms):
        total = None
        for coef, value in terms:
            if abs(coef) > 1e-12:
                term = float(coef) * value
                total = term if total is None else total + term
        return total

    out = [None] * 5
    for i in range(2):
        s = combine([(0.5 * (mat[i, k] - mat[i, 4 - k]), odd[k]) for k in range(2)])
        d = combine([(0.5 * (mat[i, k] + mat[i, 4 - k]), even[k]) for k in range(2)] + [(mat[i, 2], x[2])])
        out[i] = s + d
        out[4 - i] = s - d
    out[2] = combine([(mat[2, k], odd[k]) for k in range(2)])
    return out


def split(value):
    high = value.astype(BF16)
    return high, (value - high.astype(F32)).astype(BF16)


def dot(a, b):
    return lax.dot_general(a, b, (((1,), (0,)), ((), ())), preferred_element_type=F32)


def body(
    adj, vel, fwd, shear, inv_rad, inv_mass, counts, rec_elem, rec_force, table,
    out_v, out_w, out_k,
    v, w, f, tab, shraw, sh, irv, irb, imv, imn, imb, cnt, rel, rfv,
    ua, ud, fa, fd, q, z, kern, cc, cprev, cnext, mask,
    zbuf, zid, g0, g1, ebuf,
    lsem, tsem, osem, hs, hr, zs, zr, zis, zir, g0s, g0r, g1s, g1r, es, er, cs, cr,
):
    me = lax.axis_index("dom")
    mz, my, mx, mc = me // 32, (me // 8) % 4, (me // 2) % 4, me % 2
    nxt = (me + 1) % NDEV
    prv = (me + NDEV - 1) % NDEV
    zpeer = [((mz + k) % NZ) * 32 + me % 32 for k in range(1, NZ)]
    xpeer = [me - mx * 2 + ((mx + k) % NX) * 2 for k in range(1, NX)]
    ypeer = [me - my * 8 + ((my + k) % NY) * 8 for k in range(1, NY)]
    core = me + 1 - 2 * mc

    def local(src, dst, k):
        copy = pltpu.make_async_copy(src, dst, lsem.at[k])
        copy.start()
        return copy

    c_rf = local(rec_force, rfv, 0)
    c_rel = local(rec_elem, rel, 1)
    c_cnt = local(counts, cnt, 2)
    c_adj = [local(adj.at[:, :, pl.ds(LANES * c, LANES)], v.at[c, pl.ds(0, 4)], 3 + c) for c in range(4)]
    c_tab = []
    for k in range(8):
        copy = pltpu.make_async_copy(table.at[k], tab.at[k], tsem.at[k])
        c_tab.append(copy)
    for k in range(4):
        c_tab[k].start()
    c_f0 = [local(fwd.at[0, :, :, pl.ds(LANES * c, LANES)], f.at[0, c, pl.ds(0, 4)], 7 + c) for c in range(4)]
    c_ir = local(inv_rad, irv, 11)
    c_im = local(inv_mass, imv, 12)
    c_sh = local(shear, shraw, 13)
    for k in range(4, 8):
        c_tab[k].start()
    c_vel = [local(vel.at[:, :, pl.ds(LANES * c, LANES)], w.at[c, pl.ds(0, 4)], 14 + c) for c in range(4)]
    c_f1 = [local(fwd.at[1, :, :, pl.ds(LANES * c, LANES)], f.at[1, c, pl.ds(0, 4)], 18 + c) for c in range(4)]

    barrier = pltpu.get_barrier_semaphore()
    peers = zpeer + xpeer + ypeer + [core, nxt, prv]
    for peer in peers:
        pl.semaphore_signal(barrier, inc=1, device_id=(peer,), device_id_type=MESH)

    lane = lax.broadcasted_iota(jnp.int32, (8, WIDTH), 1)
    sub = lax.broadcasted_iota(jnp.int32, (8, WIDTH), 0)
    lane1 = lax.broadcasted_iota(jnp.int32, (1, LANES), 1)
    c_rf.wait()
    for s in range(2):
        for c in range(4):
            zbuf[pl.ds(mz * 8 + s * 4 + c, 1), :] = rfv[0, s : s + 1, LANES * c : LANES * (c + 1)]
    c_rel.wait()
    own_id = jnp.full((1, LANES), rel[0], jnp.int32).astype(F32) + 1.0
    zid[mz] = jnp.where(lane1 // 16 == mz, own_id, 0.0)

    pl.semaphore_wait(barrier, len(peers))

    def remote(src, dst, ssem, rsem, dev):
        copy = pltpu.make_async_remote_copy(
            src_ref=src, dst_ref=dst, send_sem=ssem, recv_sem=rsem, device_id=(dev,), device_id_type=MESH
        )
        copy.start()
        return copy

    zrow = pl.multiple_of(mz * 8, 8)
    z_copies = []
    for k in range(NZ - 1):
        z_copies.append(remote(zbuf.at[pl.ds(zrow, 8)], zbuf.at[pl.ds(zrow, 8)], zs.at[k], zr.at[k], zpeer[k]))
        z_copies.append(remote(zid.at[mz], zid.at[mz], zis.at[k], zir.at[k], zpeer[k]))
    h_adj, h_f0, h_vel, h_f1 = [], [], [], []
    for c in range(4):
        ls = pl.ds(LANES * c, LANES)
        h_adj.append(remote(adj.at[0, :, ls], v.at[c, 4], hs.at[c], hr.at[c], prv))
    for c in range(4):
        ls = pl.ds(LANES * c, LANES)
        h_f0.append(remote(fwd.at[0, 0, :, ls], f.at[0, c, 4], hs.at[4 + c], hr.at[4 + c], prv))
    h_im = remote(inv_mass, imn, hs.at[16], hr.at[16], prv)
    for c in range(4):
        ls = pl.ds(LANES * c, LANES)
        h_vel.append(remote(vel.at[0, :, ls], w.at[c, 4], hs.at[8 + c], hr.at[8 + c], prv))
    for c in range(4):
        ls = pl.ds(LANES * c, LANES)
        h_f1.append(remote(fwd.at[1, 0, :, ls], f.at[1, c, 4], hs.at[12 + c], hr.at[12 + c], prv))

    c_cnt.wait()
    limit = jnp.zeros((8, WIDTH), jnp.int32)
    for e in range(8):
        limit = jnp.where(sub == e, cnt[e], limit)
    live = (lane % MODES < limit).astype(F32)
    mask[0] = live
    mask[1] = live * jnp.where(me == NDEV - 1, 0.0, 1.0)

    def rows(ref, i):
        m = mask[1 if i == 4 else 0]
        out = []
        for j in range(5):
            value = jnp.concatenate([ref[c, i, pl.ds(j, 8, stride=4), :] for c in range(4)], axis=1)
            out.append(value * m)
        return out

    def transform(pieces, dests, first):
        high, low = split(jnp.concatenate(pieces, axis=0))
        plain = dot(high, tab[0]) + dot(low, tab[0]) + dot(high, tab[2])
        deriv = dot(high, tab[1]) + dot(low, tab[1]) + dot(high, tab[3])
        at = 0
        for dst, dst_d, offs in dests:
            for i in offs:
                dst[5 * i : 5 * i + 5] = plain[at : at + 40].reshape(5, 8, WIDTH)
                dst_d[5 * i : 5 * i + 5] = deriv[at : at + 40].reshape(5, 8, WIDTH)
                at += 40

    def gather(ref, offs):
        out = []
        for i in offs:
            out += rows(ref, i)
        return out

    for copy in c_adj + c_f0 + c_tab[:4]:
        copy.wait()
    f0, f1 = f.at[0], f.at[1]
    inner = [0, 1, 2, 3]
    transform(gather(v, inner) + gather(f0, inner), [(ua, ud, inner), (fa, fd, inner)], True)

    for copy in z_copies:
        copy.wait()
    own = mc * 16 + my * 4 + mx
    for s, g in ((0, g0), (1, g1)):
        for c in range(4):
            g[own, c] = zbuf[pl.ds(s * 4 + c, 8, stride=8), :]
    ids = zid[0]
    for k in range(1, NZ):
        ids = ids + zid[k]
    ebuf[own] = ids
    x0 = [remote(g0.at[own], g0.at[own], g0s.at[k], g0r.at[k], xpeer[k]) for k in range(3)]
    xe = [remote(ebuf.at[own], ebuf.at[own], es.at[k], er.at[k], xpeer[k]) for k in range(3)]
    x1 = [remote(g1.at[own], g1.at[own], g1s.at[k], g1r.at[k], xpeer[k]) for k in range(3)]

    c_ir.wait()
    for n in range(25):
        irb[n] = jnp.broadcast_to(irv[:, n : n + 1], (8, LANES))
    c_sh.wait()
    for n in range(25):
        sh[n] = shraw[:, n, :]

    for copy in h_adj + h_f0:
        copy.wait()
    transform(gather(v, [4]) + gather(f0, [4]), [(ua, ud, [4]), (fa, fd, [4])], False)

    def contraction(first):
        def chunk(c, carry):
            ls = pl.ds(pl.multiple_of(c * LANES, LANES), LANES)
            for j in range(5):
                ns = [5 * k + j for k in range(5)]
                pa = apply5(DQ, [ua[n, :, ls] for n in ns])
                pf = apply5(DQ, [fa[n, :, ls] for n in ns])
                s = [sh[n, :, ls] * p for n, p in zip(ns, pa)]
                back = apply5(DQT, s)
                for k, n in enumerate(ns):
                    q[n, :, ls] = back[k]
                    term = pa[k] * pf[k]
                    kern[n, :, ls] = term if first else kern[n, :, ls] + term
            for i in range(5):
                ns = [5 * i + k for k in range(5)]
                pa = apply5(DQ, [ua[n, :, ls] for n in ns])
                pf = apply5(DQ, [fa[n, :, ls] for n in ns])
                shs = [sh[n, :, ls] for n in ns]
                back = apply5(DQT, [a * b for a, b in zip(shs, pa)])
                for k, n in enumerate(ns):
                    q[n, :, ls] += back[k]
                    ir = irb[n]
                    p3 = ir * ud[n, :, ls]
                    kern[n, :, ls] += pa[k] * pf[k] + p3 * (ir * fd[n, :, ls])
                    z[n, :, ls] = ir * shs[k] * p3
            return carry

        lax.fori_loop(0, CHUNKS, chunk, 0)

    contraction(True)

    quad = pl.ds(pl.multiple_of(mc * 16 + my * 4, 4), 4)
    for copy in x0 + xe:
        copy.wait()
    y0 = [remote(g0.at[quad], g0.at[quad], g0s.at[3 + k], g0r.at[3 + k], ypeer[k]) for k in range(3)]
    ye = [remote(ebuf.at[quad], ebuf.at[quad], es.at[3 + k], er.at[3 + k], ypeer[k]) for k in range(3)]
    for copy in x1:
        copy.wait()
    y1 = [remote(g1.at[quad], g1.at[quad], g1s.at[3 + k], g1r.at[3 + k], ypeer[k]) for k in range(3)]

    for copy in c_tab[4:]:
        copy.wait()

    def back_rows(step, offs):
        rows_q = [q[5 * i : 5 * i + 5].reshape(40, WIDTH) for i in offs]
        rows_z = [z[5 * i : 5 * i + 5].reshape(40, WIDTH) for i in offs]
        qh, ql = split(jnp.concatenate(rows_q, axis=0))
        zh, zl = split(jnp.concatenate(rows_z, axis=0))
        total = dot(qh, tab[4]) + dot(ql, tab[4]) + dot(qh, tab[6])
        total = total + (dot(zh, tab[5]) + dot(zl, tab[5]) + dot(zh, tab[7]))
        m = mask[0]
        for at, i in enumerate(offs):
            cc[step, 5 * i : 5 * i + 5] = total[40 * at : 40 * at + 40].reshape(5, 8, WIDTH) * m[None]

    def image(step, i):
        parts = [cc[step, 5 * i + j] for j in range(5)]
        if i == 0:
            keep = jnp.where(me == 0, 0.0, 1.0)
            parts = [a + keep * cprev[step, j] for j, a in enumerate(parts)]
        if i == 4:
            parts = [a + cnext[j] for j, a in enumerate(parts)]
        return parts

    def wide(value):
        return jnp.concatenate([value] * 4, axis=1)

    def update(step, i, source=None):
        parts = image(step, i)
        turned = pltpu.roll(parts[4], 1, 0)
        cols = [parts[0] + jnp.where(sub == 0, 0.0, turned), parts[1], parts[2], parts[3]]
        for j in range(4):
            gain = DTIME * wide(imb[5 * i + j])
            load = -cols[j] if (source is None or j != 2) else source - cols[j]
            step_w = gain * load
            for c in range(4):
                at = pl.ds(j, 8, stride=4)
                new_w = w[c, i, at, :] + step_w[:, LANES * c : LANES * (c + 1)]
                w[c, i, at, :] = new_w
                v[c, i, at, :] += DTIME * new_w
        last = turned[0:1]
        for c in range(4):
            gain = DTIME * imb[5 * i + 4][0:1]
            new_w = w[c, i, 32:33, :] - gain * last[:, LANES * c : LANES * (c + 1)]
            w[c, i, 32:33, :] = new_w
            v[c, i, 32:33, :] += DTIME * new_w

    def ends(step):
        return (
            remote(cc.at[step, pl.ds(20, 5)], cprev.at[step], cs.at[2 * step], cr.at[2 * step], nxt),
            remote(cc.at[step, pl.ds(0, 5)], cnext, cs.at[2 * step + 1], cr.at[2 * step + 1], prv)
            if step == 0
            else None,
        )

    back_rows(0, [4, 0])
    up0, down0 = ends(0)
    back_rows(0, [1, 2, 3])

    c_im.wait()
    h_im.wait()
    lane33 = lax.broadcasted_iota(jnp.int32, (8, 33), 1)
    sub33 = lax.broadcasted_iota(jnp.int32, (8, 33), 0)
    for i in range(5):
        row = imv[i : i + 1, :] if i < 4 else imn[0:1, :]
        spread = jnp.broadcast_to(row, (8, 33))
        for j in range(4):
            picked = jnp.where(lane33 == 4 * sub33 + j, spread, 0.0)
            imb[5 * i + j] = jnp.broadcast_to(jnp.sum(picked, axis=1, keepdims=True), (8, LANES))
        imb[5 * i + 4] = jnp.broadcast_to(spread[:, 32:33], (8, LANES))
    for copy in c_vel + c_f1 + h_vel + h_f1:
        copy.wait()
    for i in (1, 2, 3):
        update(0, i)
    everything = [0, 1, 2, 3, 4]
    transform(gather(f1, everything), [(fa, fd, everything)], False)

    half = pl.ds(pl.multiple_of(mc * 16, 16), 16)
    for copy in y0 + ye:
        copy.wait()
    k0 = remote(g0.at[half], g0.at[half], g0s.at[6], g0r.at[6], core)
    ke = remote(ebuf.at[half], ebuf.at[half], es.at[6], er.at[6], core)
    for copy in y1:
        copy.wait()
    k1 = remote(g1.at[half], g1.at[half], g1s.at[6], g1r.at[6], core)

    up0.wait()
    down0.wait()
    update(0, 0)
    update(0, 4)
    transform(gather(v, everything), [(ua, ud, everything)], False)

    k0.wait()
    ke.wait()
    r_lane = lax.broadcasted_iota(jnp.int32, (BLOCKS, 8, LANES), 2)
    r_sub = lax.broadcasted_iota(jnp.int32, (BLOCKS, 8, LANES), 1)
    target = (me * 8 + 1 + r_lane % 16).astype(F32)
    hit = (jnp.broadcast_to(ebuf[...], (BLOCKS, 8, LANES)) == target) & (r_lane // 16 == r_sub) & (r_lane % 16 < 8)
    onehot = jnp.where(hit, 1.0, 0.0).reshape(BLOCKS * 8, LANES).T.astype(BF16)

    def source_of(g):
        outs = []
        for c in range(4):
            high, low = split(g[:, c].reshape(BLOCKS * 8, LANES))
            total = dot(onehot, high) + dot(onehot, low)
            acc = total[0:8]
            for k in range(1, 8):
                acc = acc + total[16 * k : 16 * k + 8]
            outs.append(acc)
        return jnp.concatenate(outs, axis=1)

    kick = DTIME * wide(imb[12]) * source_of(g0)
    shift = DTIME * kick
    for c in range(4):
        at = pl.ds(2, 8, stride=4)
        w[c, 2, at, :] += kick[:, LANES * c : LANES * (c + 1)]
        v[c, 2, at, :] += shift[:, LANES * c : LANES * (c + 1)]
    high, low = split(shift * mask[0])
    ua[12] += dot(high, tab[0]) + dot(low, tab[0]) + dot(high, tab[2])
    ud[12] += dot(high, tab[1]) + dot(low, tab[1]) + dot(high, tab[3])

    contraction(False)
    back_rows(1, [4, 0])
    up1, _ = ends(1)
    for n in range(25):
        shraw[:, n, :] = kern[n]
    o_k = pltpu.make_async_copy(shraw, out_k, osem.at[0])
    o_k.start()
    back_rows(1, [1, 2, 3])
    k1.wait()
    update(1, 2, source_of(g1))
    update(1, 1)
    update(1, 3)
    up1.wait()
    update(1, 0)
    outs = [o_k]
    for c in range(4):
        ls = pl.ds(LANES * c, LANES)
        copy = pltpu.make_async_copy(v.at[c, pl.ds(0, 4)], out_v.at[:, :, ls], osem.at[1 + c])
        copy.start()
        outs.append(copy)
        copy = pltpu.make_async_copy(w.at[c, pl.ds(0, 4)], out_w.at[:, :, ls], osem.at[5 + c])
        copy.start()
        outs.append(copy)
    for copy in outs:
        copy.wait()


def per_device(adj, vel, fwd, shear, inv_rad, inv_mass, counts, rec_elem, rec_force):
    table = jnp.asarray(tables())
    node = (4, 5, 33, LANES)
    elem = (25, 8, WIDTH)
    dma = pltpu.SemaphoreType.DMA
    scratch = [
        pltpu.VMEM(node, F32),
        pltpu.VMEM(node, F32),
        pltpu.VMEM((2,) + node, F32),
        pltpu.VMEM((8, WIDTH, WIDTH), BF16),
        pltpu.VMEM((8, 25, WIDTH), F32),
        pltpu.VMEM(elem, F32),
        pltpu.VMEM((8, 25), F32),
        pltpu.VMEM((25, 8, LANES), F32),
        pltpu.VMEM((4, 33), F32),
        pltpu.VMEM((4, 33), F32),
        pltpu.VMEM((25, 8, LANES), F32),
        pltpu.SMEM((8,), jnp.int32),
        pltpu.SMEM((1,), jnp.int32),
        pltpu.VMEM((1, 2, WIDTH), F32),
        pltpu.VMEM(elem, F32),
        pltpu.VMEM(elem, F32),
        pltpu.VMEM(elem, F32),
        pltpu.VMEM(elem, F32),
        pltpu.VMEM(elem, F32),
        pltpu.VMEM(elem, F32),
        pltpu.VMEM(elem, F32),
        pltpu.VMEM((2,) + elem, F32),
        pltpu.VMEM((2, 5, 8, WIDTH), F32),
        pltpu.VMEM((5, 8, WIDTH), F32),
        pltpu.VMEM((2, 8, WIDTH), F32),
        pltpu.VMEM((64, LANES), F32),
        pltpu.VMEM((NZ, 1, LANES), F32),
        pltpu.VMEM((BLOCKS, 4, 8, LANES), F32),
        pltpu.VMEM((BLOCKS, 4, 8, LANES), F32),
        pltpu.VMEM((BLOCKS, 1, LANES), F32),
        dma((22,)),
        dma((8,)),
        dma((9,)),
        dma((17,)),
        dma((17,)),
        dma((7,)),
        dma((7,)),
        dma((7,)),
        dma((7,)),
        dma((7,)),
        dma((7,)),
        dma((7,)),
        dma((7,)),
        dma((7,)),
        dma((7,)),
        dma((4,)),
        dma((4,)),
    ]
    shapes = [
        jax.ShapeDtypeStruct((4, 33, WIDTH), F32),
        jax.ShapeDtypeStruct((4, 33, WIDTH), F32),
        jax.ShapeDtypeStruct((8, 25, WIDTH), F32),
    ]
    return pl.pallas_call(
        body,
        out_shape=shapes,
        in_specs=[pl.BlockSpec(memory_space=pl.ANY)] * 10,
        out_specs=[pl.BlockSpec(memory_space=pl.ANY)] * 3,
        scratch_shapes=scratch,
        compiler_params=pltpu.CompilerParams(
            collective_id=0, has_side_effects=True, vmem_limit_bytes=48 * 2**20
        ),
        name="adjoint_steps",
    )(adj, vel, fwd, shear, inv_rad, inv_mass, counts, rec_elem, rec_force, table)


def solution(mesh):
    in_specs = (
        P("dom", None, None),
        P("dom", None, None),
        P(None, "dom", None, None),
        P("dom", None, None),
        P("dom", None),
        P("dom", None),
        P("dom"),
        P("dom"),
        P("dom", None, None),
    )
    out_specs = (P("dom", None, None), P("dom", None, None), P("dom", None, None))
    return jax.shard_map(per_device, mesh=mesh, in_specs=in_specs, out_specs=out_specs, check_vma=False)
```

```python
import functools

import jax
import jax.numpy as jnp
import ml_dtypes
import numpy as np
from jax import lax
from jax.experimental import pallas as pl
from jax.experimental.pallas import tpu as pltpu
from jax.sharding import PartitionSpec as P

GSCALE = 0.25
DTIME = 0.25
NZ, NY, NX, NCORE = 8, 4, 4, 2
NDEV = NZ * NY * NX * NCORE
LANES = 128
CHUNKS = 4
MODES = 256
WIDTH = 512
MESH = pl.DeviceIdType.MESH
F32 = jnp.float32
BF16 = jnp.bfloat16


def gll_derivative():
    points = np.array([-1.0, -np.sqrt(3.0 / 7.0), 0.0, np.sqrt(3.0 / 7.0), 1.0])
    legendre = (35.0 * points**4 - 30.0 * points**2 + 3.0) / 8.0
    matrix = np.zeros((5, 5))
    for row in range(5):
        for col in range(5):
            if row != col:
                matrix[row, col] = legendre[row] / (legendre[col] * (points[row] - points[col]))
    matrix[0, 0] = -5.0
    matrix[4, 4] = 5.0
    return matrix


DQ = GSCALE * gll_derivative()
DQT = DQ.T


def tables():
    mode = np.arange(MODES)[:, None]
    angle = 2.0 * np.pi * (mode * np.arange(WIDTH)[None, :] % WIDTH) / WIDTH
    scale = 1.0 / np.sqrt(MODES)
    cos, sin = np.cos(angle) * scale, np.sin(angle) * scale
    plain = np.concatenate([cos, -sin], axis=0)
    deriv = np.concatenate([-mode * sin, -mode * cos], axis=0)

    def parts(table):
        high = table.astype(ml_dtypes.bfloat16)
        low = (table - high.astype(np.float64)).astype(ml_dtypes.bfloat16)
        return high, low

    ph, plo = parts(plain)
    dh, dlo = parts(deriv)
    return np.stack([ph, dh, plo, dlo, ph.T, dh.T, plo.T, dlo.T])


def apply5(mat, x):
    even = [x[0] + x[4], x[1] + x[3]]
    odd = [x[0] - x[4], x[1] - x[3]]

    def combine(terms):
        total = None
        for coef, value in terms:
            if abs(coef) > 1e-12:
                term = float(coef) * value
                total = term if total is None else total + term
        return total

    out = [None] * 5
    for i in range(2):
        s = combine([(0.5 * (mat[i, k] - mat[i, 4 - k]), odd[k]) for k in range(2)])
        d = combine([(0.5 * (mat[i, k] + mat[i, 4 - k]), even[k]) for k in range(2)] + [(mat[i, 2], x[2])])
        out[i] = s + d
        out[4 - i] = s - d
    out[2] = combine([(mat[2, k], odd[k]) for k in range(2)])
    return out


def split(value):
    high = value.astype(BF16)
    return high, (value - high.astype(F32)).astype(BF16)


def dot(a, b):
    return lax.dot_general(a, b, (((1,), (0,)), ((), ())), preferred_element_type=F32)


def body(
    adj, vel, fwd, shear, inv_rad, inv_mass, counts, rec_elem, rec_force, table,
    out_v, out_w, out_k,
    v, w, f, tab, sh, irv, irb, imv, imn, imb, cnt, rel,
    ua, ud, fa, fd, fa1, fd1, q, z, kern, cc, cprev, cnext, mask, halo, edge,
    cross, crossn, cb, zraw, zid, g0, g1, ebuf, psend, precv, pown,
    lsem, tsem, osem, hs, hr, zs, zr, zis, zir, g0s, g0r, g1s, g1r, es, er, cs, cr, ps, pr,
):
    me = lax.axis_index("dom")
    mz, my, mx, mc = me // 32, (me // 8) % 4, (me // 2) % 4, me % 2
    nxt = (me + 1) % NDEV
    prv = (me + NDEV - 1) % NDEV
    zpeer = [((mz + k) % NZ) * 32 + me % 32 for k in range(1, NZ)]
    shifts = [(0, 2), (2, 0), (2, 2), (1, 2), (2, 1), (3, 2), (2, 3), (1, 1), (1, 3), (3, 1), (3, 3), (0, 1), (1, 0), (0, 3), (3, 0)]
    ppeer = [mz * 32 + ((my + j) % NY) * 8 + ((mx + k) % NX) * 2 + mc for j, k in shifts]
    core = me + 1 - 2 * mc

    def local(src, dst, k):
        copy = pltpu.make_async_copy(src, dst, lsem.at[k])
        copy.start()
        return copy

    c_rf = local(rec_force.at[0], zraw.at[mz], 0)
    c_rel = local(rec_elem, rel, 1)
    c_cnt = local(counts, cnt, 2)
    c_adj = [local(adj.at[:, :, pl.ds(LANES * c, LANES)], v.at[c], 3 + c) for c in range(4)]
    c_tab = []
    for k in range(8):
        copy = pltpu.make_async_copy(table.at[k], tab.at[k], tsem.at[k])
        c_tab.append(copy)
    for k in range(4):
        c_tab[k].start()
    c_f0 = [local(fwd.at[0, :, :, pl.ds(LANES * c, LANES)], f.at[0, c], 7 + c) for c in range(4)]
    c_ir = local(inv_rad, irv, 11)
    c_im = local(inv_mass, imv, 12)
    c_sh = local(shear, sh, 13)
    for k in range(4, 8):
        c_tab[k].start()
    c_vel = [local(vel.at[:, :, pl.ds(LANES * c, LANES)], w.at[c], 14 + c) for c in range(4)]
    c_f1 = [local(fwd.at[1, :, :, pl.ds(LANES * c, LANES)], f.at[1, c], 18 + c) for c in range(4)]

    vv = [v.at[c].reshape(132, LANES) for c in range(4)]
    wv = [w.at[c].reshape(132, LANES) for c in range(4)]
    fv = [[f.at[s, c].reshape(132, LANES) for c in range(4)] for s in range(2)]

    def at(i, j):
        return pl.ds(4 * j + i, 8, stride=16)

    barrier = pltpu.get_barrier_semaphore()
    peers = zpeer + ppeer + [core]
    for peer in peers:
        pl.semaphore_signal(barrier, inc=1, device_id=(peer,), device_id_type=MESH)
    above, below = me < NDEV - 1, me > 0

    @pl.when(above)
    def _():
        pl.semaphore_signal(barrier, inc=1, device_id=(nxt,), device_id_type=MESH)

    @pl.when(below)
    def _():
        pl.semaphore_signal(barrier, inc=1, device_id=(prv,), device_id_type=MESH)

    lane = lax.broadcasted_iota(jnp.int32, (8, WIDTH), 1)
    sub = lax.broadcasted_iota(jnp.int32, (8, WIDTH), 0)
    lane1 = lax.broadcasted_iota(jnp.int32, (1, LANES), 1)
    missing = (me + NDEV - 1) // NDEV - me // (NDEV - 1)
    pl.semaphore_wait(barrier, len(peers) + 1 + missing)

    def remote(src, dst, ssem, rsem, dev):
        copy = pltpu.make_async_remote_copy(
            src_ref=src, dst_ref=dst, send_sem=ssem, recv_sem=rsem, device_id=(dev,), device_id_type=MESH
        )
        copy.start()
        return copy

    class Link:
        def __init__(self, src, dst, k, up, sems):
            self.sends, self.takes = (above, below) if up else (below, above)
            self.copy = pltpu.make_async_remote_copy(
                src_ref=src,
                dst_ref=dst,
                send_sem=sems[0].at[k],
                recv_sem=sems[1].at[k],
                device_id=(nxt if up else prv,),
                device_id_type=MESH,
            )

            @pl.when(self.sends)
            def _():
                self.copy.start()

        def wait(self):
            @pl.when(self.takes)
            def _():
                self.copy.wait_recv()

            @pl.when(self.sends)
            def _():
                self.copy.wait_send()

    z_copies = [remote(rec_force.at[0], zraw.at[mz], zs.at[k], zr.at[k], zpeer[k]) for k in range(NZ - 1)]
    c_rel.wait()
    own_id = jnp.full((1, LANES), rel[0], jnp.int32).astype(F32)
    zid[mz] = jnp.where(lane1 // 16 == mz, own_id, 0.0)
    id_copies = [remote(zid.at[mz], zid.at[mz], zis.at[k], zir.at[k], zpeer[k]) for k in range(NZ - 1)]

    def send_row(view, copies, k):
        for copy in copies:
            copy.wait()
        for j in range(5):
            for c in range(4):
                edge[k, j, :, LANES * c : LANES * (c + 1)] = view[c][at(0, j), :]
        return Link(edge.at[k], halo.at[k], k, False, (hs, hr))

    h_adj = send_row(vv, c_adj, 0)
    h_f0 = send_row(fv[0], c_f0, 1)
    h_im = Link(inv_mass, imn, 4, False, (hs, hr))

    c_cnt.wait()
    limit = jnp.zeros((8, WIDTH), jnp.int32)
    for e in range(8):
        limit = jnp.where(sub == e, cnt[e], limit)
    live = (lane % MODES < limit).astype(F32)
    mask[0] = live
    mask[1] = live * jnp.where(me == NDEV - 1, 0.0, 1.0)

    @pl.when(me == NDEV - 1)
    def _():
        halo[...] = jnp.zeros(halo.shape, F32)
        cnext[...] = jnp.zeros(cnext.shape, F32)
        imn[...] = jnp.zeros(imn.shape, F32)

    @pl.when(me == 0)
    def _():
        cprev[...] = jnp.zeros(cprev.shape, F32)
        crossn[...] = jnp.zeros(crossn.shape, F32)


    def rows(view, k, i):
        out = []
        for j in range(5):
            if i == 4:
                out.append(halo[k, j] * mask[1])
            else:
                out.append(jnp.concatenate([view[c][at(i, j), :] for c in range(4)], axis=1) * mask[0])
        return out

    def transform(pieces, dests):
        high, low = split(jnp.concatenate(pieces, axis=0))
        plain = dot(high, tab[0]) + dot(low, tab[0]) + dot(high, tab[2])
        deriv = dot(high, tab[1]) + dot(low, tab[1]) + dot(high, tab[3])
        at = 0
        for dst, dst_d, offs in dests:
            for i in offs:
                dst[5 * i : 5 * i + 5] = plain[at : at + 40].reshape(5, 8, WIDTH)
                dst_d[5 * i : 5 * i + 5] = deriv[at : at + 40].reshape(5, 8, WIDTH)
                at += 40

    def gather(view, k, offs):
        out = []
        for i in offs:
            out += rows(view, k, i)
        return out

    for copy in c_tab[:4]:
        copy.wait()
    inner = [0, 1, 2, 3]
    transform(gather(vv, 0, inner) + gather(fv[0], 1, inner), [(ua, ud, inner), (fa, fd, inner)])

    h_f1 = send_row(fv[1], c_f1, 3)
    h_vel = send_row(wv, c_vel, 2)
    transform(gather(fv[1], 3, inner), [(fa1, fd1, inner)])
    def wide(value):
        return jnp.concatenate([value] * 4, axis=1)

    c_ir.wait()
    for n in range(25):
        irb[n] = jnp.broadcast_to(irv[:, n : n + 1], (8, LANES))
    c_sh.wait()
    c_im.wait()
    lane33 = lax.broadcasted_iota(jnp.int32, (8, 33), 1)
    sub33 = lax.broadcasted_iota(jnp.int32, (8, 33), 0)
    def mass(i):
        row = imv[i : i + 1, :] if i < 4 else imn[0:1, :]
        spread = jnp.broadcast_to(row, (8, 33))
        for j in range(4 if i < 4 else 5):
            picked = jnp.where(lane33 == 4 * sub33 + j, spread, 0.0)
            imb[5 * i + j] = jnp.broadcast_to(jnp.sum(picked, axis=1, keepdims=True), (8, LANES))
        if i < 4:
            imb[5 * i + 4] = jnp.broadcast_to(spread[:, 32:33], (8, LANES))
    for i in range(4):
        mass(i)
    for k in range(5):
        cb[k] = sum(float(DQ[i, k] * DQ[i, 2]) * sh[5 * i + 2] for i in (0, 1, 3, 4))
        cb[5 + k] = sum(float(DQ[i, k] * DQ[i, 2]) * sh[10 + i] for i in (0, 1, 3, 4))
    cross[0] = (DTIME * DTIME) * wide(imb[12]) * mask[0]
    cross[1] = cb[4]
    cross[2] = mask[0]
    h_cross = Link(cross, crossn, 5, True, (hs, hr))

    h_adj.wait()
    h_f0.wait()
    transform(gather(vv, 0, [4]) + gather(fv[0], 1, [4]), [(ua, ud, [4]), (fa, fd, [4])])

    def contraction(first, fa, fd):
        def chunk(c, carry):
            ls = pl.ds(pl.multiple_of(c * LANES, LANES), LANES)
            for j in range(5):
                ns = [5 * k + j for k in range(5)]
                pa = apply5(DQ, [ua[n, :, ls] for n in ns])
                pf = apply5(DQ, [fa[n, :, ls] for n in ns])
                s = [sh[n, :, ls] * p for n, p in zip(ns, pa)]
                back = apply5(DQT, s)
                for k, n in enumerate(ns):
                    q[n, :, ls] = back[k]
                    term = pa[k] * pf[k]
                    kern[n, :, ls] = term if first else kern[n, :, ls] + term
            for i in range(5):
                ns = [5 * i + k for k in range(5)]
                pa = apply5(DQ, [ua[n, :, ls] for n in ns])
                pf = apply5(DQ, [fa[n, :, ls] for n in ns])
                shs = [sh[n, :, ls] for n in ns]
                back = apply5(DQT, [a * b for a, b in zip(shs, pa)])
                for k, n in enumerate(ns):
                    q[n, :, ls] += back[k]
                    ir = irb[n]
                    p3 = ir * ud[n, :, ls]
                    kern[n, :, ls] += pa[k] * pf[k] + p3 * (ir * fd[n, :, ls])
                    z[n, :, ls] = ir * shs[k] * p3
            return carry

        lax.fori_loop(0, CHUNKS, chunk, 0)

    contraction(True, fa, fd)

    for copy in c_tab[4:]:
        copy.wait()

    def back_rows(step, offs):
        rows_q = [q[5 * i : 5 * i + 5].reshape(40, WIDTH) for i in offs]
        rows_z = [z[5 * i : 5 * i + 5].reshape(40, WIDTH) for i in offs]
        qh, ql = split(jnp.concatenate(rows_q, axis=0))
        zh, zl = split(jnp.concatenate(rows_z, axis=0))
        total = dot(qh, tab[4]) + dot(ql, tab[4]) + dot(qh, tab[6])
        total = total + (dot(zh, tab[5]) + dot(zl, tab[5]) + dot(zh, tab[7]))
        m = mask[0]
        for at, i in enumerate(offs):
            cc[step, 5 * i : 5 * i + 5] = total[40 * at : 40 * at + 40].reshape(5, 8, WIDTH) * m[None]

    def image(step, i):
        parts = [cc[step, 5 * i + j] for j in range(5)]
        if i == 0:
            parts = [a + cprev[step, j] for j, a in enumerate(parts)]
        return parts

    def update(step, i):
        parts = image(step, i)
        turned = pltpu.roll(parts[4], 1, 0)
        cols = [parts[0] + jnp.where(sub == 0, 0.0, turned), parts[1], parts[2], parts[3]]
        for j in range(4):
            gain = DTIME * wide(imb[5 * i + j])
            step_w = gain * cols[j]
            for c in range(4):
                new_w = wv[c][at(i, j), :] - step_w[:, LANES * c : LANES * (c + 1)]
                wv[c][at(i, j), :] = new_w
                vv[c][at(i, j), :] += DTIME * new_w
        last = turned[0:1]
        for c in range(4):
            row = slice(128 + i, 129 + i)
            gain = DTIME * imb[5 * i + 4][0:1]
            new_w = wv[c][row, :] - gain * last[:, LANES * c : LANES * (c + 1)]
            wv[c][row, :] = new_w
            vv[c][row, :] += DTIME * new_w

    def update_halo():
        parts = [cc[0, 20 + j] + cnext[j] for j in range(5)]
        left = pltpu.roll(parts[4], 1, 0)
        right = pltpu.roll(parts[0], 7, 0)
        cols = [parts[0] + jnp.where(sub == 0, 0.0, left), parts[1], parts[2], parts[3]]
        cols.append(parts[4] + jnp.where(sub == 7, 0.0, right))
        for j in range(5):
            halo[0, j] += DTIME * (halo[2, j] - DTIME * wide(imb[20 + j]) * cols[j])

    def ends(step):
        up = Link(cc.at[step, pl.ds(20, 5)], cprev.at[step], 2 * step, True, (cs, cr))
        return up, Link(cc.at[step, pl.ds(0, 5)], cnext, 1, False, (cs, cr)) if step == 0 else None

    back_rows(0, [4, 0])
    up0, down0 = ends(0)
    own = my * 4 + mx
    c_rf.wait()
    for copy in z_copies:
        copy.wait()
    for c in range(4):
        g0[own, c] = zraw[:, 0, LANES * c : LANES * (c + 1)]
    p0 = [remote(g0.at[own], g0.at[own], g0s.at[k], g0r.at[k], ppeer[k]) for k in range(15)]
    for copy in id_copies:
        copy.wait()
    ids = zid[0]
    for k in range(1, NZ):
        ids = ids + zid[k]
    ebuf[own] = ids
    pe = [remote(ebuf.at[own], ebuf.at[own], es.at[k], er.at[k], ppeer[k]) for k in range(15)]
    for c in range(4):
        g1[own, c] = zraw[:, 1, LANES * c : LANES * (c + 1)]
    p1 = [remote(g1.at[own], g1.at[own], g1s.at[k], g1r.at[k], ppeer[k]) for k in range(15)]

    back_rows(0, [1, 2, 3])

    for i in (1, 2, 3):
        update(0, i)
    transform(gather(vv, 0, [1, 2, 3]), [(ua, ud, [1, 2, 3])])
    h_im.wait()
    mass(4)
    h_vel.wait()
    h_f1.wait()
    up0.wait()
    down0.wait()
    update(0, 0)
    update_halo()
    transform(gather(vv, 0, [0, 4]) + gather(fv[1], 3, [4]), [(ua, ud, [0, 4]), (fa1, fd1, [4])])

    contraction(False, fa1, fd1)
    back_rows(1, [4, 0])
    up1, _ = ends(1)
    outs = []

    def out_kernel(first, count, k):
        piece = pl.ds(first, count)
        copy = pltpu.make_async_copy(kern.at[piece], out_k.at[piece], osem.at[k])
        copy.start()
        outs.append(copy)

    for k, (first, count) in enumerate([(0, 2), (3, 4), (8, 2), (15, 2), (18, 4), (23, 2)]):
        out_kernel(first, count, k)
    back_rows(1, [1, 2, 3])
    for i in (1, 2, 3):
        update(1, i)
    for copy in p0 + pe:
        copy.wait()
    half = NY * NX
    r_lane = lax.broadcasted_iota(jnp.int32, (half, 8, LANES), 2)
    r_sub = lax.broadcasted_iota(jnp.int32, (half, 8, LANES), 1)
    group = r_lane // 16 == r_sub
    ids_all = jnp.broadcast_to(ebuf[...], (half, 8, LANES))

    def onehot(dev):
        target = ((dev - 1) * 8 + r_lane % 16).astype(F32)
        hit = (ids_all == target) & group
        return jnp.where(hit, 1.0, 0.0).reshape(half * 8, LANES).T.astype(BF16)

    pick = jnp.concatenate([onehot(core), onehot(me)], axis=0)

    def sums(g, k):
        for c in range(4):
            high, low = split(g[:, c].reshape(half * 8, LANES))
            total = dot(pick, high) + dot(pick, low)
            for d, ref in ((0, psend), (LANES, pown)):
                acc = total[d : d + 16]
                for t in range(1, 8):
                    acc = acc + total[d + 16 * t : d + 16 * t + 16]
                ref[k, :, LANES * c : LANES * (c + 1)] = acc
        return remote(psend.at[k], precv.at[k], ps.at[k], pr.at[k], core)

    k0 = sums(g0, 0)
    for copy in p1:
        copy.wait()
    k1 = sums(g1, 1)

    up1.wait()
    update(1, 0)
    h_cross.wait()

    k0.wait()
    source0 = pown[0] + precv[0]
    kick = DTIME * wide(imb[12]) * source0[8:16]
    high, low = split(jnp.concatenate([kick * (DTIME * mask[0]), crossn[0] * source0[0:8]], axis=0))
    plain = dot(high, tab[0]) + dot(low, tab[0]) + dot(high, tab[2])
    deriv = (dot(high, tab[1]) + dot(low, tab[1]) + dot(high, tab[3]))[0:8]
    before, plain = plain[8:16], plain[0:8]
    turn = wide(irb[12])
    col_f = apply5(DQ, [fa1[5 * k + 2] for k in range(5)])
    row_f = apply5(DQ, [fa1[10 + k] for k in range(5)])
    for k in (0, 1, 3, 4):
        kern[5 * k + 2] += float(DQ[k, 2]) * plain * col_f[k]
        kern[10 + k] += float(DQ[k, 2]) * plain * row_f[k]
    kern[12] += (turn * deriv) * (turn * fd1[12])
    for k, (first, count) in enumerate([(2, 1), (7, 1), (10, 5), (17, 1), (22, 1)]):
        out_kernel(first, count, 6 + k)
    terms = [cb[k] * plain for k in (0, 1, 3)] + [cb[5 + k] * plain for k in (0, 1, 3, 4)]
    terms += [crossn[1] * before, (cb[2] + cb[7]) * plain]
    high, low = split(jnp.concatenate(terms, axis=0))
    back = dot(high, tab[4]) + dot(low, tab[4]) + dot(high, tab[6])
    high, low = split(turn * turn * sh[12] * deriv)
    extra = dot(high, tab[5]) + dot(low, tab[5]) + dot(high, tab[7])
    b = [back[8 * k : 8 * k + 8] * mask[0] for k in range(7)]
    before = back[56:64] * crossn[2]
    middle = (back[64:72] + extra) * mask[0]
    turned = pltpu.roll(b[6], 1, 0)
    fix = {(0, 2): b[0] + before, (1, 2): b[1], (3, 2): b[2]}
    fix[(2, 0)] = b[3] + jnp.where(sub == 0, 0.0, turned)
    fix[(2, 1)], fix[(2, 3)], fix[(2, 2)] = b[4], b[5], middle
    k1.wait()
    kick1 = DTIME * wide(imb[12]) * (pown[1, 8:16] + precv[1, 8:16])
    for (i, j), value in fix.items():
        move = -(DTIME * wide(imb[5 * i + j])) * value
        shift = DTIME * move
        if (i, j) == (2, 2):
            move = move + kick + kick1
            shift = DTIME * (move + kick)
        for c in range(4):
            ls = slice(LANES * c, LANES * (c + 1))
            wv[c][at(i, j), :] += move[:, ls]
            vv[c][at(i, j), :] += shift[:, ls]
    for c in range(4):
        move = -(DTIME * imb[14][0:1]) * turned[0:1, LANES * c : LANES * (c + 1)]
        wv[c][130:131, :] += move
        vv[c][130:131, :] += DTIME * move
    for c in range(4):
        ls = pl.ds(LANES * c, LANES)
        copy = pltpu.make_async_copy(v.at[c], out_v.at[:, :, ls], osem.at[11 + c])
        copy.start()
        outs.append(copy)
        copy = pltpu.make_async_copy(w.at[c], out_w.at[:, :, ls], osem.at[15 + c])
        copy.start()
        outs.append(copy)
    for copy in outs:
        copy.wait()


def finish(a, b, c, oa, ob, oc, ta, tb, tc, sem):
    triples = [(a, ta, oa), (b, tb, ob), (c, tc, oc)]
    reads = [pltpu.make_async_copy(x, t, sem.at[k]) for k, (x, t, _) in enumerate(triples)]
    writes = [pltpu.make_async_copy(t, y, sem.at[3 + k]) for k, (_, t, y) in enumerate(triples)]
    for copy in reads:
        copy.start()
    for read, write in zip(reads, writes):
        read.wait()
        write.start()
    for copy in writes:
        copy.wait()


def per_device(adj, vel, fwd, shear, inv_rad, inv_mass, counts, rec_elem, rec_force):
    table = jnp.asarray(tables())
    node = (4, 33, 4, LANES)
    elem = (25, 8, WIDTH)
    dma = pltpu.SemaphoreType.DMA
    scratch = [
        pltpu.VMEM(node, F32),
        pltpu.VMEM(node, F32),
        pltpu.VMEM((2,) + node, F32),
        pltpu.VMEM((8, WIDTH, WIDTH), BF16),
        pltpu.VMEM(elem, F32),
        pltpu.VMEM((8, 25), F32),
        pltpu.VMEM((25, 8, LANES), F32),
        pltpu.VMEM((4, 33), F32),
        pltpu.VMEM((4, 33), F32),
        pltpu.VMEM((25, 8, LANES), F32),
        pltpu.SMEM((8,), jnp.int32),
        pltpu.SMEM((1,), jnp.int32),
        pltpu.VMEM(elem, F32),
        pltpu.VMEM(elem, F32),
        pltpu.VMEM(elem, F32),
        pltpu.VMEM(elem, F32),
        pltpu.VMEM(elem, F32),
        pltpu.VMEM(elem, F32),
        pltpu.VMEM(elem, F32),
        pltpu.VMEM(elem, F32),
        pltpu.VMEM(elem, F32),
        pltpu.VMEM((2,) + elem, F32),
        pltpu.VMEM((2, 5, 8, WIDTH), F32),
        pltpu.VMEM((5, 8, WIDTH), F32),
        pltpu.VMEM((2, 8, WIDTH), F32),
        pltpu.VMEM((4, 5, 8, WIDTH), F32),
        pltpu.VMEM((4, 5, 8, WIDTH), F32),
        pltpu.VMEM((3, 8, WIDTH), F32),
        pltpu.VMEM((3, 8, WIDTH), F32),
        pltpu.VMEM((10, 8, WIDTH), F32),
        pltpu.VMEM((NZ, 2, WIDTH), F32),
        pltpu.VMEM((NZ, 1, LANES), F32),
        pltpu.VMEM((NY * NX, 4, 8, LANES), F32),
        pltpu.VMEM((NY * NX, 4, 8, LANES), F32),
        pltpu.VMEM((NY * NX, 1, LANES), F32),
        pltpu.VMEM((2, 16, WIDTH), F32),
        pltpu.VMEM((2, 16, WIDTH), F32),
        pltpu.VMEM((2, 16, WIDTH), F32),
        dma((22,)),
        dma((8,)),
        dma((19,)),
        dma((6,)),
        dma((6,)),
        dma((7,)),
        dma((7,)),
        dma((7,)),
        dma((7,)),
        dma((15,)),
        dma((15,)),
        dma((15,)),
        dma((15,)),
        dma((15,)),
        dma((15,)),
        dma((4,)),
        dma((4,)),
        dma((2,)),
        dma((2,)),
    ]
    shapes = [
        jax.ShapeDtypeStruct((33, 4, WIDTH), F32),
        jax.ShapeDtypeStruct((33, 4, WIDTH), F32),
        jax.ShapeDtypeStruct((25, 8, WIDTH), F32),
    ]
    new_disp, new_vel, kernel = pl.pallas_call(
        body,
        out_shape=shapes,
        in_specs=[pl.BlockSpec(memory_space=pltpu.HBM)] * 10,
        out_specs=[pl.BlockSpec(memory_space=pltpu.HBM)] * 3,
        scratch_shapes=scratch,
        compiler_params=pltpu.CompilerParams(
            collective_id=0, has_side_effects=True, vmem_limit_bytes=63 * 2**20
        ),
        name="adjoint_steps",
    )(
        jnp.transpose(adj, (1, 0, 2)),
        jnp.transpose(vel, (1, 0, 2)),
        jnp.transpose(fwd, (0, 2, 1, 3)),
        jnp.transpose(shear, (1, 0, 2)),
        inv_rad,
        inv_mass,
        counts,
        rec_elem,
        rec_force,
        table,
    )
    outs = pl.pallas_call(
        finish,
        out_shape=shapes,
        in_specs=[pl.BlockSpec(memory_space=pltpu.HBM)] * 3,
        out_specs=[pl.BlockSpec(memory_space=pltpu.HBM)] * 3,
        scratch_shapes=[pltpu.VMEM(t.shape, F32) for t in shapes] + [dma((6,))],
        compiler_params=pltpu.CompilerParams(vmem_limit_bytes=63 * 2**20),
        name="results",
    )(new_disp, new_vel, kernel)
    return tuple(jnp.transpose(out, (1, 0, 2)) for out in outs)


def solution(mesh):
    in_specs = (
        P("dom", None, None),
        P("dom", None, None),
        P(None, "dom", None, None),
        P("dom", None, None),
        P("dom", None),
        P("dom", None),
        P("dom"),
        P("dom"),
        P("dom", None, None),
    )
    out_specs = (P("dom", None, None), P("dom", None, None), P("dom", None, None))
    return jax.shard_map(per_device, mesh=mesh, in_specs=in_specs, out_specs=out_specs, check_vma=False)
```

```python
import functools

import jax
import jax.numpy as jnp
import ml_dtypes
import numpy as np
from jax import lax
from jax.experimental import pallas as pl
from jax.experimental.pallas import tpu as pltpu
from jax.sharding import PartitionSpec as P

GSCALE = 0.25
DTIME = 0.25
NZ, NY, NX, NCORE = 8, 4, 4, 2
NDEV = NZ * NY * NX * NCORE
LANES = 128
CHUNKS = 4
MODES = 256
WIDTH = 512
MESH = pl.DeviceIdType.MESH
F32 = jnp.float32
BF16 = jnp.bfloat16


def gll_derivative():
    points = np.array([-1.0, -np.sqrt(3.0 / 7.0), 0.0, np.sqrt(3.0 / 7.0), 1.0])
    legendre = (35.0 * points**4 - 30.0 * points**2 + 3.0) / 8.0
    matrix = np.zeros((5, 5))
    for row in range(5):
        for col in range(5):
            if row != col:
                matrix[row, col] = legendre[row] / (legendre[col] * (points[row] - points[col]))
    matrix[0, 0] = -5.0
    matrix[4, 4] = 5.0
    return matrix


DQ = GSCALE * gll_derivative()
DQT = DQ.T


def tables():
    mode = np.arange(MODES)[:, None]
    angle = 2.0 * np.pi * (mode * np.arange(WIDTH)[None, :] % WIDTH) / WIDTH
    scale = 1.0 / np.sqrt(MODES)
    cos, sin = np.cos(angle) * scale, np.sin(angle) * scale
    plain = np.concatenate([cos, -sin], axis=0)
    deriv = np.concatenate([-mode * sin, -mode * cos], axis=0)

    def parts(table):
        high = table.astype(ml_dtypes.bfloat16)
        low = (table - high.astype(np.float64)).astype(ml_dtypes.bfloat16)
        return high, low

    ph, plo = parts(plain)
    dh, dlo = parts(deriv)
    return np.stack([ph, dh, plo, dlo, ph.T, dh.T, plo.T, dlo.T])


def apply5(mat, x):
    even = [x[0] + x[4], x[1] + x[3]]
    odd = [x[0] - x[4], x[1] - x[3]]

    def combine(terms):
        total = None
        for coef, value in terms:
            if abs(coef) > 1e-12:
                term = float(coef) * value
                total = term if total is None else total + term
        return total

    out = [None] * 5
    for i in range(2):
        s = combine([(0.5 * (mat[i, k] - mat[i, 4 - k]), odd[k]) for k in range(2)])
        d = combine([(0.5 * (mat[i, k] + mat[i, 4 - k]), even[k]) for k in range(2)] + [(mat[i, 2], x[2])])
        out[i] = s + d
        out[4 - i] = s - d
    out[2] = combine([(mat[2, k], odd[k]) for k in range(2)])
    return out


def split(value):
    high = value.astype(BF16)
    return high, (value - high.astype(F32)).astype(BF16)


def dot(a, b):
    return lax.dot_general(a, b, (((1,), (0,)), ((), ())), preferred_element_type=F32)


def times(x, *parts):
    rows = x.shape[0]
    high = x.astype(BF16)
    both = jnp.concatenate([x, x - high.astype(F32)], axis=0).astype(BF16)
    out = []
    for table_high, table_low in parts:
        first = dot(both, table_high)
        out.append(first[:rows] + first[rows:] + dot(high, table_low))
    return out


def body(
    adj, vel, fwd, shear, inv_rad, inv_mass, counts, rec_elem, rec_force, table,
    out_v, out_w, out_k,
    v, w, f, tab, sh, irv, irb, imv, imn, imb, cnt, rel,
    ua, ud, fa, fd, fa1, fd1, q, z, kern, cc, cprev, cnext, mask, halo, edge,
    cross, crossn, cb, zraw, zid, g0, g1, ebuf, psend, precv, pown,
    lsem, tsem, osem, hs, hr, zs, zr, zis, zir, g0s, g0r, g1s, g1r, es, er, cs, cr, ps, pr, relay,
):
    me = lax.axis_index("dom")
    mz, my, mx, mc = me // 32, (me // 8) % 4, (me // 2) % 4, me % 2
    nxt = (me + 1) % NDEV
    prv = (me + NDEV - 1) % NDEV
    zpeer = [((mz + k) % NZ) * 32 + me % 32 for k in range(1, NZ)]
    shifts = [(0, 2), (2, 0), (2, 2), (1, 2), (2, 1), (3, 2), (2, 3), (1, 1), (1, 3), (3, 1), (3, 3), (0, 1), (1, 0), (0, 3), (3, 0)]
    ppeer = [mz * 32 + ((my + j) % NY) * 8 + ((mx + k) % NX) * 2 + mc for j, k in shifts]
    xpeer = [me - mx * 2 + ((mx + k) % NX) * 2 for k in range(1, NX)]
    ypeer = [me - my * 8 + ((my + k) % NY) * 8 for k in range(1, NY)]
    core = me + 1 - 2 * mc

    barrier = pltpu.get_barrier_semaphore()
    peers = zpeer + xpeer + ypeer + [core]
    for peer in peers:
        pl.semaphore_signal(barrier, inc=1, device_id=(peer,), device_id_type=MESH)
    above, below = me < NDEV - 1, me > 0

    @pl.when(above)
    def _():
        pl.semaphore_signal(barrier, inc=1, device_id=(nxt,), device_id_type=MESH)

    @pl.when(below)
    def _():
        pl.semaphore_signal(barrier, inc=1, device_id=(prv,), device_id_type=MESH)

    def local(src, dst, k):
        copy = pltpu.make_async_copy(src, dst, lsem.at[k])
        copy.start()
        return copy

    c_rf = local(rec_force.at[0], zraw.at[mz], 0)
    c_rel = local(rec_elem, rel, 1)
    c_cnt = local(counts, cnt, 2)
    c_adj = [local(adj.at[:, :, pl.ds(LANES * c, LANES)], v.at[c], 3 + c) for c in range(4)]
    c_tab = [
        pltpu.make_async_copy(table.at[pl.ds(4 * k, 4)], tab.at[pl.ds(4 * k, 4)], tsem.at[k]) for k in range(2)
    ]
    c_tab[0].start()
    c_f0 = [local(fwd.at[0, :, :, pl.ds(LANES * c, LANES)], f.at[0, c], 7 + c) for c in range(4)]
    c_ir = local(inv_rad, irv, 11)
    c_im = local(inv_mass, imv, 12)
    c_sh = local(shear, sh, 13)
    c_tab[1].start()
    c_vel = [local(vel.at[:, :, pl.ds(LANES * c, LANES)], w.at[c], 14 + c) for c in range(4)]
    c_f1 = [local(fwd.at[1, :, :, pl.ds(LANES * c, LANES)], f.at[1, c], 18 + c) for c in range(4)]

    vv = [v.at[c].reshape(132, LANES) for c in range(4)]
    wv = [w.at[c].reshape(132, LANES) for c in range(4)]
    fv = [[f.at[s, c].reshape(132, LANES) for c in range(4)] for s in range(2)]

    def at(i, j):
        return pl.ds(4 * j + i, 8, stride=16)

    lane = lax.broadcasted_iota(jnp.int32, (8, WIDTH), 1)
    sub = lax.broadcasted_iota(jnp.int32, (8, WIDTH), 0)
    lane1 = lax.broadcasted_iota(jnp.int32, (1, LANES), 1)
    missing = (me + NDEV - 1) // NDEV - me // (NDEV - 1)
    pl.semaphore_wait(barrier, len(peers) + 1 + missing)

    def remote(src, dst, ssem, rsem, dev):
        copy = pltpu.make_async_remote_copy(
            src_ref=src, dst_ref=dst, send_sem=ssem, recv_sem=rsem, device_id=(dev,), device_id_type=MESH
        )
        copy.start()
        return copy

    class Link:
        def __init__(self, src, dst, k, up, sems):
            self.sends, self.takes = (above, below) if up else (below, above)
            self.copy = pltpu.make_async_remote_copy(
                src_ref=src,
                dst_ref=dst,
                send_sem=sems[0].at[k],
                recv_sem=sems[1].at[k],
                device_id=(nxt if up else prv,),
                device_id_type=MESH,
            )

            @pl.when(self.sends)
            def _():
                self.copy.start()

        def wait(self):
            @pl.when(self.takes)
            def _():
                self.copy.wait_recv()

            @pl.when(self.sends)
            def _():
                self.copy.wait_send()

    z_copies = [remote(rec_force.at[0], zraw.at[mz], zs.at[k], zr.at[k], zpeer[k]) for k in range(NZ - 1)]
    c_rel.wait()
    own_id = jnp.full((1, LANES), rel[0], jnp.int32).astype(F32)
    zid[mz] = jnp.where(lane1 // 16 == mz, own_id, 0.0)
    id_copies = [remote(zid.at[mz], zid.at[mz], zis.at[k], zir.at[k], zpeer[k]) for k in range(NZ - 1)]

    def send_row(view, copies, k):
        for copy in copies:
            copy.wait()
        for j in range(5):
            for c in range(4):
                edge[k, j, :, LANES * c : LANES * (c + 1)] = view[c][at(0, j), :]
        return Link(edge.at[k], halo.at[k], k, False, (hs, hr))

    h_adj = send_row(vv, c_adj, 0)
    h_f0 = send_row(fv[0], c_f0, 1)
    h_im = Link(inv_mass, imn, 4, False, (hs, hr))

    for peer in xpeer:
        pl.semaphore_signal(relay, inc=1, device_id=(peer,), device_id_type=MESH)

    c_cnt.wait()
    limit = jnp.zeros((8, WIDTH), jnp.int32)
    for e in range(8):
        limit = jnp.where(sub == e, cnt[e], limit)
    live = (lane % MODES < limit).astype(F32)
    mask[0] = live
    mask[1] = live * jnp.where(me == NDEV - 1, 0.0, 1.0)

    @pl.when(me == NDEV - 1)
    def _():
        halo[...] = jnp.zeros(halo.shape, F32)
        cnext[...] = jnp.zeros(cnext.shape, F32)
        imn[...] = jnp.zeros(imn.shape, F32)

    @pl.when(me == 0)
    def _():
        cprev[...] = jnp.zeros(cprev.shape, F32)
        crossn[...] = jnp.zeros(crossn.shape, F32)


    def rows(view, k, i):
        out = []
        for j in range(5):
            if i == 4:
                out.append(halo[k, j] * mask[1])
            else:
                out.append(jnp.concatenate([view[c][at(i, j), :] for c in range(4)], axis=1) * mask[0])
        return out

    def transform(pieces, dests):
        plain, deriv = times(jnp.concatenate(pieces, axis=0), (tab[0], tab[2]), (tab[1], tab[3]))
        at = 0
        for dst, dst_d, offs in dests:
            for i in offs:
                dst[5 * i : 5 * i + 5] = plain[at : at + 40].reshape(5, 8, WIDTH)
                dst_d[5 * i : 5 * i + 5] = deriv[at : at + 40].reshape(5, 8, WIDTH)
                at += 40

    def gather(view, k, offs):
        out = []
        for i in offs:
            out += rows(view, k, i)
        return out

    c_tab[0].wait()
    inner = [0, 1, 2, 3]
    transform(gather(vv, 0, inner) + gather(fv[0], 1, inner), [(ua, ud, inner), (fa, fd, inner)])

    h_f1 = send_row(fv[1], c_f1, 3)
    h_vel = send_row(wv, c_vel, 2)
    transform(gather(fv[1], 3, inner), [(fa1, fd1, inner)])
    def wide(value):
        return jnp.concatenate([value] * 4, axis=1)

    c_ir.wait()
    for n in range(25):
        irb[n] = jnp.broadcast_to(irv[:, n : n + 1], (8, LANES))
    c_sh.wait()
    c_im.wait()
    lane33 = lax.broadcasted_iota(jnp.int32, (8, 33), 1)
    sub33 = lax.broadcasted_iota(jnp.int32, (8, 33), 0)
    def mass(i):
        row = imv[i : i + 1, :] if i < 4 else imn[0:1, :]
        spread = jnp.broadcast_to(row, (8, 33))
        for j in range(4 if i < 4 else 5):
            picked = jnp.where(lane33 == 4 * sub33 + j, spread, 0.0)
            imb[5 * i + j] = jnp.broadcast_to(jnp.sum(picked, axis=1, keepdims=True), (8, LANES))
        if i < 4:
            imb[5 * i + 4] = jnp.broadcast_to(spread[:, 32:33], (8, LANES))
    for i in range(4):
        mass(i)
    for k in range(5):
        cb[k] = sum(float(DQ[i, k] * DQ[i, 2]) * sh[5 * i + 2] for i in (0, 1, 3, 4))
        cb[5 + k] = sum(float(DQ[i, k] * DQ[i, 2]) * sh[10 + i] for i in (0, 1, 3, 4))
    cross[0] = (DTIME * DTIME) * wide(imb[12]) * mask[0]
    cross[1] = cb[4]
    cross[2] = mask[0]
    h_cross = Link(cross, crossn, 5, True, (hs, hr))

    h_adj.wait()
    h_f0.wait()
    transform(gather(vv, 0, [4]) + gather(fv[0], 1, [4]), [(ua, ud, [4]), (fa, fd, [4])])

    def contraction(first, fa, fd, offs):
        def chunk(c, carry):
            ls = pl.ds(pl.multiple_of(c * LANES, LANES), LANES)
            for j in range(5) if 0 in offs else ():
                ns = [5 * k + j for k in range(5)]
                pa = apply5(DQ, [ua[n, :, ls] for n in ns])
                pf = apply5(DQ, [fa[n, :, ls] for n in ns])
                s = [sh[n, :, ls] * p for n, p in zip(ns, pa)]
                back = apply5(DQT, s)
                for k, n in enumerate(ns):
                    q[n, :, ls] = back[k]
                    term = pa[k] * pf[k]
                    kern[n, :, ls] = term if first else kern[n, :, ls] + term
            for i in offs:
                ns = [5 * i + k for k in range(5)]
                pa = apply5(DQ, [ua[n, :, ls] for n in ns])
                pf = apply5(DQ, [fa[n, :, ls] for n in ns])
                shs = [sh[n, :, ls] for n in ns]
                back = apply5(DQT, [a * b for a, b in zip(shs, pa)])
                for k, n in enumerate(ns):
                    q[n, :, ls] += back[k]
                    ir = irb[n]
                    p3 = ir * ud[n, :, ls]
                    kern[n, :, ls] += pa[k] * pf[k] + p3 * (ir * fd[n, :, ls])
                    z[n, :, ls] = ir * shs[k] * p3
            return carry

        lax.fori_loop(0, CHUNKS, chunk, 0)

    contraction(True, fa, fd, (0, 4))

    c_tab[1].wait()

    def back_rows(step, offs):
        rows_q = [q[5 * i : 5 * i + 5].reshape(40, WIDTH) for i in offs]
        rows_z = [z[5 * i : 5 * i + 5].reshape(40, WIDTH) for i in offs]
        (total,) = times(jnp.concatenate(rows_q, axis=0), (tab[4], tab[6]))
        (azimuthal,) = times(jnp.concatenate(rows_z, axis=0), (tab[5], tab[7]))
        total = total + azimuthal
        m = mask[0]
        for at, i in enumerate(offs):
            cc[step, 5 * i : 5 * i + 5] = total[40 * at : 40 * at + 40].reshape(5, 8, WIDTH) * m[None]

    def image(step, i):
        parts = [cc[step, 5 * i + j] for j in range(5)]
        if i == 0:
            parts = [a + cprev[step, j] for j, a in enumerate(parts)]
        return parts

    def update(step, i):
        parts = image(step, i)
        turned = pltpu.roll(parts[4], 1, 0)
        cols = [parts[0] + jnp.where(sub == 0, 0.0, turned), parts[1], parts[2], parts[3]]
        for j in range(4):
            gain = DTIME * wide(imb[5 * i + j])
            step_w = gain * cols[j]
            for c in range(4):
                new_w = wv[c][at(i, j), :] - step_w[:, LANES * c : LANES * (c + 1)]
                wv[c][at(i, j), :] = new_w
                vv[c][at(i, j), :] += DTIME * new_w
        last = turned[0:1]
        for c in range(4):
            row = slice(128 + i, 129 + i)
            gain = DTIME * imb[5 * i + 4][0:1]
            new_w = wv[c][row, :] - gain * last[:, LANES * c : LANES * (c + 1)]
            wv[c][row, :] = new_w
            vv[c][row, :] += DTIME * new_w

    def update_halo():
        parts = [cc[0, 20 + j] + cnext[j] for j in range(5)]
        left = pltpu.roll(parts[4], 1, 0)
        right = pltpu.roll(parts[0], 7, 0)
        cols = [parts[0] + jnp.where(sub == 0, 0.0, left), parts[1], parts[2], parts[3]]
        cols.append(parts[4] + jnp.where(sub == 7, 0.0, right))
        for j in range(5):
            halo[0, j] += DTIME * (halo[2, j] - DTIME * wide(imb[20 + j]) * cols[j])

    def ends(step):
        up = Link(cc.at[step, pl.ds(20, 5)], cprev.at[step], 2 * step, True, (cs, cr))
        return up, Link(cc.at[step, pl.ds(0, 5)], cnext, 1, False, (cs, cr)) if step == 0 else None

    back_rows(0, [4, 0])
    up0, down0 = ends(0)
    own = my * 4 + mx
    c_rf.wait()
    for copy in z_copies:
        copy.wait()
    for copy in id_copies:
        copy.wait()
    pl.semaphore_wait(relay, len(xpeer))
    ids = zid[0]
    for k in range(1, NZ):
        ids = ids + zid[k]
    ebuf[own] = ids
    pe = [remote(ebuf.at[own], ebuf.at[own], es.at[k], er.at[k], ppeer[k]) for k in range(15)]
    for c in range(4):
        g0[own, c] = zraw[:, 0, LANES * c : LANES * (c + 1)]
    p0 = [remote(g0.at[own], g0.at[own], g0s.at[k], g0r.at[k], ppeer[k]) for k in range(15)]
    for c in range(4):
        g1[own, c] = zraw[:, 1, LANES * c : LANES * (c + 1)]
    p1 = [remote(g1.at[own], g1.at[own], g1s.at[k], g1r.at[k], ppeer[k]) for k in range(15)]

    contraction(True, fa, fd, (1, 2, 3))
    back_rows(0, [1, 2, 3])

    for i in (1, 2, 3):
        update(0, i)
    transform(gather(vv, 0, [1, 2, 3]), [(ua, ud, [1, 2, 3])])
    h_im.wait()
    mass(4)
    h_vel.wait()
    h_f1.wait()
    up0.wait()
    down0.wait()
    update(0, 0)
    update_halo()
    transform(gather(vv, 0, [0, 4]) + gather(fv[1], 3, [4]), [(ua, ud, [0, 4]), (fa1, fd1, [4])])

    contraction(False, fa1, fd1, (0, 4))
    back_rows(1, [4, 0])
    up1, _ = ends(1)
    contraction(False, fa1, fd1, (1, 2, 3))
    outs = []

    def out_kernel(first, count, k):
        piece = pl.ds(first, count)
        copy = pltpu.make_async_copy(kern.at[piece], out_k.at[piece], osem.at[k])
        copy.start()
        outs.append(copy)

    for k, (first, count) in enumerate([(0, 2), (3, 4), (8, 2), (15, 2), (18, 4), (23, 2)]):
        out_kernel(first, count, k)
    back_rows(1, [1, 2, 3])
    for i in (1, 2, 3):
        update(1, i)
    for copy in pe:
        copy.wait()
    half = NY * NX
    r_lane = lax.broadcasted_iota(jnp.int32, (half, 8, LANES), 2)
    r_sub = lax.broadcasted_iota(jnp.int32, (half, 8, LANES), 1)
    group = r_lane // 16 == r_sub
    ids_all = jnp.broadcast_to(ebuf[...], (half, 8, LANES))

    def onehot(dev):
        target = ((dev - 1) * 8 + r_lane % 16).astype(F32)
        hit = (ids_all == target) & group
        return jnp.where(hit, 1.0, 0.0).reshape(half * 8, LANES).T.astype(BF16)

    pick = jnp.concatenate([onehot(core), onehot(me)], axis=0)

    for copy in p0:
        copy.wait()

    def sums(g, k):
        for c in range(4):
            high, low = split(g[:, c].reshape(half * 8, LANES))
            total = dot(pick, high) + dot(pick, low)
            for d, ref in ((0, psend), (LANES, pown)):
                acc = total[d : d + 16]
                for t in range(1, 8):
                    acc = acc + total[d + 16 * t : d + 16 * t + 16]
                ref[k, :, LANES * c : LANES * (c + 1)] = acc
        return remote(psend.at[k], precv.at[k], ps.at[k], pr.at[k], core)

    k0 = sums(g0, 0)
    for copy in p1:
        copy.wait()
    k1 = sums(g1, 1)
    up1.wait()
    update(1, 0)
    h_cross.wait()

    turn = wide(irb[12])
    col_f = apply5(DQ, [fa1[5 * k + 2] for k in range(5)])
    row_f = apply5(DQ, [fa1[10 + k] for k in range(5)])
    k0.wait()
    source0 = pown[0] + precv[0]
    kick = DTIME * wide(imb[12]) * source0[8:16]
    moved = jnp.concatenate([kick * (DTIME * mask[0]), crossn[0] * source0[0:8]], axis=0)
    plain, deriv = times(moved, (tab[0], tab[2]), (tab[1], tab[3]))
    before, plain, deriv = plain[8:16], plain[0:8], deriv[0:8]
    for k in (0, 1, 3, 4):
        kern[5 * k + 2] += float(DQ[k, 2]) * plain * col_f[k]
        kern[10 + k] += float(DQ[k, 2]) * plain * row_f[k]
    kern[12] += (turn * deriv) * (turn * fd1[12])
    for k, (first, count) in enumerate([(2, 1), (7, 1), (10, 5), (17, 1), (22, 1)]):
        out_kernel(first, count, 6 + k)
    terms = [cb[k] * plain for k in (0, 1, 3)] + [cb[5 + k] * plain for k in (0, 1, 3, 4)]
    terms += [crossn[1] * before, (cb[2] + cb[7]) * plain]
    (back,) = times(jnp.concatenate(terms, axis=0), (tab[4], tab[6]))
    (extra,) = times(turn * turn * sh[12] * deriv, (tab[5], tab[7]))
    b = [back[8 * k : 8 * k + 8] * mask[0] for k in range(7)]
    before = back[56:64] * crossn[2]
    middle = (back[64:72] + extra) * mask[0]
    turned = pltpu.roll(b[6], 1, 0)
    fix = {(0, 2): b[0] + before, (1, 2): b[1], (3, 2): b[2]}
    fix[(2, 0)] = b[3] + jnp.where(sub == 0, 0.0, turned)
    fix[(2, 1)], fix[(2, 3)], fix[(2, 2)] = b[4], b[5], middle
    k1.wait()
    kick1 = DTIME * wide(imb[12]) * (pown[1, 8:16] + precv[1, 8:16])
    for (i, j), value in fix.items():
        move = -(DTIME * wide(imb[5 * i + j])) * value
        shift = DTIME * move
        if (i, j) == (2, 2):
            move = move + kick + kick1
            shift = DTIME * (move + kick)
        for c in range(4):
            ls = slice(LANES * c, LANES * (c + 1))
            wv[c][at(i, j), :] += move[:, ls]
            vv[c][at(i, j), :] += shift[:, ls]
    for c in range(4):
        move = -(DTIME * imb[14][0:1]) * turned[0:1, LANES * c : LANES * (c + 1)]
        wv[c][130:131, :] += move
        vv[c][130:131, :] += DTIME * move
    for c in range(4):
        ls = pl.ds(LANES * c, LANES)
        copy = pltpu.make_async_copy(v.at[c], out_v.at[:, :, ls], osem.at[11 + c])
        copy.start()
        outs.append(copy)
        copy = pltpu.make_async_copy(w.at[c], out_w.at[:, :, ls], osem.at[15 + c])
        copy.start()
        outs.append(copy)
    for copy in outs:
        copy.wait()


def finish(a, b, c, oa, ob, oc, ta, tb, tc, sem):
    triples = [(a, ta, oa), (b, tb, ob), (c, tc, oc)]
    reads = [pltpu.make_async_copy(x, t, sem.at[k]) for k, (x, t, _) in enumerate(triples)]
    writes = [pltpu.make_async_copy(t, y, sem.at[3 + k]) for k, (_, t, y) in enumerate(triples)]
    for copy in reads:
        copy.start()
    for read, write in zip(reads, writes):
        read.wait()
        write.start()
    for copy in writes:
        copy.wait()


def per_device(adj, vel, fwd, shear, inv_rad, inv_mass, counts, rec_elem, rec_force):
    table = jnp.asarray(tables())
    node = (4, 33, 4, LANES)
    elem = (25, 8, WIDTH)
    dma = pltpu.SemaphoreType.DMA
    scratch = [
        pltpu.VMEM(node, F32),
        pltpu.VMEM(node, F32),
        pltpu.VMEM((2,) + node, F32),
        pltpu.VMEM((8, WIDTH, WIDTH), BF16),
        pltpu.VMEM(elem, F32),
        pltpu.VMEM((8, 25), F32),
        pltpu.VMEM((25, 8, LANES), F32),
        pltpu.VMEM((4, 33), F32),
        pltpu.VMEM((4, 33), F32),
        pltpu.VMEM((25, 8, LANES), F32),
        pltpu.SMEM((8,), jnp.int32),
        pltpu.SMEM((1,), jnp.int32),
        pltpu.VMEM(elem, F32),
        pltpu.VMEM(elem, F32),
        pltpu.VMEM(elem, F32),
        pltpu.VMEM(elem, F32),
        pltpu.VMEM(elem, F32),
        pltpu.VMEM(elem, F32),
        pltpu.VMEM(elem, F32),
        pltpu.VMEM(elem, F32),
        pltpu.VMEM(elem, F32),
        pltpu.VMEM((2,) + elem, F32),
        pltpu.VMEM((2, 5, 8, WIDTH), F32),
        pltpu.VMEM((5, 8, WIDTH), F32),
        pltpu.VMEM((2, 8, WIDTH), F32),
        pltpu.VMEM((4, 5, 8, WIDTH), F32),
        pltpu.VMEM((4, 5, 8, WIDTH), F32),
        pltpu.VMEM((3, 8, WIDTH), F32),
        pltpu.VMEM((3, 8, WIDTH), F32),
        pltpu.VMEM((10, 8, WIDTH), F32),
        pltpu.VMEM((NZ, 2, WIDTH), F32),
        pltpu.VMEM((NZ, 1, LANES), F32),
        pltpu.VMEM((NY * NX, 4, 8, LANES), F32),
        pltpu.VMEM((NY * NX, 4, 8, LANES), F32),
        pltpu.VMEM((NY * NX, 1, LANES), F32),
        pltpu.VMEM((2, 16, WIDTH), F32),
        pltpu.VMEM((2, 16, WIDTH), F32),
        pltpu.VMEM((2, 16, WIDTH), F32),
        dma((22,)),
        dma((2,)),
        dma((19,)),
        dma((6,)),
        dma((6,)),
        dma((7,)),
        dma((7,)),
        dma((7,)),
        dma((7,)),
        dma((15,)),
        dma((15,)),
        dma((15,)),
        dma((15,)),
        dma((15,)),
        dma((15,)),
        dma((4,)),
        dma((4,)),
        dma((2,)),
        dma((2,)),
        pltpu.SemaphoreType.REGULAR,
    ]
    shapes = [
        jax.ShapeDtypeStruct((33, 4, WIDTH), F32),
        jax.ShapeDtypeStruct((33, 4, WIDTH), F32),
        jax.ShapeDtypeStruct((25, 8, WIDTH), F32),
    ]
    new_disp, new_vel, kernel = pl.pallas_call(
        body,
        out_shape=shapes,
        in_specs=[pl.BlockSpec(memory_space=pltpu.HBM)] * 10,
        out_specs=[pl.BlockSpec(memory_space=pltpu.HBM)] * 3,
        scratch_shapes=scratch,
        compiler_params=pltpu.CompilerParams(
            collective_id=0, has_side_effects=True, vmem_limit_bytes=63 * 2**20
        ),
        name="adjoint_steps",
    )(
        jnp.transpose(adj, (1, 0, 2)),
        jnp.transpose(vel, (1, 0, 2)),
        jnp.transpose(fwd, (0, 2, 1, 3)),
        jnp.transpose(shear, (1, 0, 2)),
        inv_rad,
        inv_mass,
        counts,
        rec_elem,
        rec_force,
        table,
    )
    outs = pl.pallas_call(
        finish,
        out_shape=shapes,
        in_specs=[pl.BlockSpec(memory_space=pltpu.HBM)] * 3,
        out_specs=[pl.BlockSpec(memory_space=pltpu.HBM)] * 3,
        scratch_shapes=[pltpu.VMEM(t.shape, F32) for t in shapes] + [dma((6,))],
        compiler_params=pltpu.CompilerParams(vmem_limit_bytes=63 * 2**20),
        name="results",
    )(new_disp, new_vel, kernel)
    return tuple(jnp.transpose(out, (1, 0, 2)) for out in outs)


def solution(mesh):
    in_specs = (
        P("dom", None, None),
        P("dom", None, None),
        P(None, "dom", None, None),
        P("dom", None, None),
        P("dom", None),
        P("dom", None),
        P("dom"),
        P("dom"),
        P("dom", None, None),
    )
    out_specs = (P("dom", None, None), P("dom", None, None), P("dom", None, None))
    return jax.shard_map(per_device, mesh=mesh, in_specs=in_specs, out_specs=out_specs, check_vma=False)
```

```python
import functools

import jax
import jax.numpy as jnp
import ml_dtypes
import numpy as np
from jax import lax
from jax.experimental import pallas as pl
from jax.experimental.pallas import tpu as pltpu
from jax.sharding import PartitionSpec as P

GSCALE = 0.25
DTIME = 0.25
NZ, NY, NX, NCORE = 8, 4, 4, 2
NDEV = NZ * NY * NX * NCORE
LANES = 128
CHUNKS = 4
MODES = 256
WIDTH = 512
MESH = pl.DeviceIdType.MESH
F32 = jnp.float32
BF16 = jnp.bfloat16


def gll_derivative():
    points = np.array([-1.0, -np.sqrt(3.0 / 7.0), 0.0, np.sqrt(3.0 / 7.0), 1.0])
    legendre = (35.0 * points**4 - 30.0 * points**2 + 3.0) / 8.0
    matrix = np.zeros((5, 5))
    for row in range(5):
        for col in range(5):
            if row != col:
                matrix[row, col] = legendre[row] / (legendre[col] * (points[row] - points[col]))
    matrix[0, 0] = -5.0
    matrix[4, 4] = 5.0
    return matrix


DQ = GSCALE * gll_derivative()
DQT = DQ.T


def tables():
    mode = np.arange(MODES)[:, None]
    angle = 2.0 * np.pi * (mode * np.arange(WIDTH)[None, :] % WIDTH) / WIDTH
    scale = 1.0 / np.sqrt(MODES)
    cos, sin = np.cos(angle) * scale, np.sin(angle) * scale
    plain = np.concatenate([cos, -sin], axis=0)
    deriv = np.concatenate([-mode * sin, -mode * cos], axis=0)

    def parts(table):
        high = table.astype(ml_dtypes.bfloat16)
        low = (table - high.astype(np.float64)).astype(ml_dtypes.bfloat16)
        return high, low

    ph, plo = parts(plain)
    dh, dlo = parts(deriv)
    return np.stack([ph, dh, plo, dlo, ph.T, dh.T, plo.T, dlo.T])


def apply5(mat, x):
    even = [x[0] + x[4], x[1] + x[3]]
    odd = [x[0] - x[4], x[1] - x[3]]

    def combine(terms):
        total = None
        for coef, value in terms:
            if abs(coef) > 1e-12:
                term = float(coef) * value
                total = term if total is None else total + term
        return total

    out = [None] * 5
    for i in range(2):
        s = combine([(0.5 * (mat[i, k] - mat[i, 4 - k]), odd[k]) for k in range(2)])
        d = combine([(0.5 * (mat[i, k] + mat[i, 4 - k]), even[k]) for k in range(2)] + [(mat[i, 2], x[2])])
        out[i] = s + d
        out[4 - i] = s - d
    out[2] = combine([(mat[2, k], odd[k]) for k in range(2)])
    return out


def split(value):
    high = value.astype(BF16)
    return high, (value - high.astype(F32)).astype(BF16)


def dot(a, b):
    return lax.dot_general(a, b, (((1,), (0,)), ((), ())), preferred_element_type=F32)


def times(x, *parts):
    rows = x.shape[0]
    high = x.astype(BF16)
    both = jnp.concatenate([x, x - high.astype(F32)], axis=0).astype(BF16)
    out = []
    for table_high, table_low in parts:
        first = dot(both, table_high)
        out.append(first[:rows] + first[rows:] + dot(high, table_low))
    return out


def body(
    adj, vel, fwd, shear, inv_rad, inv_mass, counts, rec_elem, rec_force, table,
    out_v, out_w, kern,
    v, w, f, tab, sh, irv, irb, imv, imn, imb, cnt, rel,
    ua, ud, fa, fd, fa1, fd1, q, z, cc, cprev, cnext, mask, halo, edge,
    cross, crossn, cb, zraw, zid, g0, g1, ebuf, psend, precv, pown,
    lsem, tsem, osem, hs, hr, zs, zr, zis, zir, g0s, g0r, g1s, g1r, es, er, cs, cr, ps, pr, relay,
):
    me = lax.axis_index("dom")
    mz, my, mx, mc = me // 32, (me // 8) % 4, (me // 2) % 4, me % 2
    nxt = (me + 1) % NDEV
    prv = (me + NDEV - 1) % NDEV
    zpeer = [((mz + k) % NZ) * 32 + me % 32 for k in range(1, NZ)]
    shifts = [(0, 2), (2, 0), (2, 2), (1, 2), (2, 1), (3, 2), (2, 3), (1, 1), (1, 3), (3, 1), (3, 3), (0, 1), (1, 0), (0, 3), (3, 0)]
    ppeer = [mz * 32 + ((my + j) % NY) * 8 + ((mx + k) % NX) * 2 + mc for j, k in shifts]
    xpeer = [me - mx * 2 + ((mx + k) % NX) * 2 for k in range(1, NX)]
    ypeer = [me - my * 8 + ((my + k) % NY) * 8 for k in range(1, NY)]
    core = me + 1 - 2 * mc

    barrier = pltpu.get_barrier_semaphore()
    peers = zpeer + xpeer + ypeer + [core]
    for peer in peers:
        pl.semaphore_signal(barrier, inc=1, device_id=(peer,), device_id_type=MESH)
    above, below = me < NDEV - 1, me > 0

    @pl.when(above)
    def _():
        pl.semaphore_signal(barrier, inc=1, device_id=(nxt,), device_id_type=MESH)

    @pl.when(below)
    def _():
        pl.semaphore_signal(barrier, inc=1, device_id=(prv,), device_id_type=MESH)

    def local(src, dst, k):
        copy = pltpu.make_async_copy(src, dst, lsem.at[k])
        copy.start()
        return copy

    c_rf = local(rec_force.at[0], zraw.at[mz], 0)
    c_rel = local(rec_elem, rel, 1)
    c_cnt = local(counts, cnt, 2)
    c_adj = [local(adj.at[:, :, pl.ds(LANES * c, LANES)], v.at[c], 3 + c) for c in range(4)]
    c_tab = [
        pltpu.make_async_copy(table.at[pl.ds(4 * k, 4)], tab.at[pl.ds(4 * k, 4)], tsem.at[k]) for k in range(2)
    ]
    c_tab[0].start()
    c_f0 = [local(fwd.at[0, :, :, pl.ds(LANES * c, LANES)], f.at[0, c], 7 + c) for c in range(4)]
    c_ir = local(inv_rad, irv, 11)
    c_im = local(inv_mass, imv, 12)
    c_sh = local(shear, sh, 13)
    c_tab[1].start()
    c_vel = [local(vel.at[:, :, pl.ds(LANES * c, LANES)], w.at[c], 14 + c) for c in range(4)]
    c_f1 = [local(fwd.at[1, :, :, pl.ds(LANES * c, LANES)], f.at[1, c], 18 + c) for c in range(4)]

    vv = [v.at[c].reshape(132, LANES) for c in range(4)]
    wv = [w.at[c].reshape(132, LANES) for c in range(4)]
    fv = [[f.at[s, c].reshape(132, LANES) for c in range(4)] for s in range(2)]

    def at(i, j):
        return pl.ds(4 * j + i, 8, stride=16)

    lane = lax.broadcasted_iota(jnp.int32, (8, WIDTH), 1)
    sub = lax.broadcasted_iota(jnp.int32, (8, WIDTH), 0)
    lane1 = lax.broadcasted_iota(jnp.int32, (1, LANES), 1)
    missing = (me + NDEV - 1) // NDEV - me // (NDEV - 1)
    pl.semaphore_wait(barrier, len(peers) + 1 + missing)

    def remote(src, dst, ssem, rsem, dev):
        copy = pltpu.make_async_remote_copy(
            src_ref=src, dst_ref=dst, send_sem=ssem, recv_sem=rsem, device_id=(dev,), device_id_type=MESH
        )
        copy.start()
        return copy

    class Link:
        def __init__(self, src, dst, k, up, sems):
            self.sends, self.takes = (above, below) if up else (below, above)
            self.copy = pltpu.make_async_remote_copy(
                src_ref=src,
                dst_ref=dst,
                send_sem=sems[0].at[k],
                recv_sem=sems[1].at[k],
                device_id=(nxt if up else prv,),
                device_id_type=MESH,
            )

            @pl.when(self.sends)
            def _():
                self.copy.start()

        def wait(self):
            @pl.when(self.takes)
            def _():
                self.copy.wait_recv()

            @pl.when(self.sends)
            def _():
                self.copy.wait_send()

    z_copies = [remote(rec_force.at[0], zraw.at[mz], zs.at[k], zr.at[k], zpeer[k]) for k in range(NZ - 1)]
    c_rel.wait()
    own_id = jnp.full((1, LANES), rel[0], jnp.int32).astype(F32)
    zid[mz] = jnp.where(lane1 // 16 == mz, own_id, 0.0)
    id_copies = [remote(zid.at[mz], zid.at[mz], zis.at[k], zir.at[k], zpeer[k]) for k in range(NZ - 1)]

    def send_row(view, copies, k):
        for copy in copies:
            copy.wait()
        for j in range(5):
            for c in range(4):
                edge[k, j, :, LANES * c : LANES * (c + 1)] = view[c][at(0, j), :]
        return Link(edge.at[k], halo.at[k], k, False, (hs, hr))

    h_adj = send_row(vv, c_adj, 0)
    h_f0 = send_row(fv[0], c_f0, 1)
    h_im = Link(inv_mass, imn, 4, False, (hs, hr))

    for peer in xpeer:
        pl.semaphore_signal(relay, inc=1, device_id=(peer,), device_id_type=MESH)

    c_cnt.wait()
    limit = jnp.zeros((8, WIDTH), jnp.int32)
    for e in range(8):
        limit = jnp.where(sub == e, cnt[e], limit)
    live = (lane % MODES < limit).astype(F32)
    mask[0] = live
    mask[1] = live * jnp.where(me == NDEV - 1, 0.0, 1.0)

    @pl.when(me == NDEV - 1)
    def _():
        halo[...] = jnp.zeros(halo.shape, F32)
        cnext[...] = jnp.zeros(cnext.shape, F32)
        imn[...] = jnp.zeros(imn.shape, F32)

    @pl.when(me == 0)
    def _():
        cprev[...] = jnp.zeros(cprev.shape, F32)
        crossn[...] = jnp.zeros(crossn.shape, F32)


    def rows(view, k, i):
        out = []
        for j in range(5):
            if i == 4:
                out.append(halo[k, j] * mask[1])
            else:
                out.append(jnp.concatenate([view[c][at(i, j), :] for c in range(4)], axis=1) * mask[0])
        return out

    def transform(pieces, dests):
        plain, deriv = times(jnp.concatenate(pieces, axis=0), (tab[0], tab[2]), (tab[1], tab[3]))
        at = 0
        for dst, dst_d, offs in dests:
            for i in offs:
                dst[5 * i : 5 * i + 5] = plain[at : at + 40].reshape(5, 8, WIDTH)
                dst_d[5 * i : 5 * i + 5] = deriv[at : at + 40].reshape(5, 8, WIDTH)
                at += 40

    def gather(view, k, offs):
        out = []
        for i in offs:
            out += rows(view, k, i)
        return out

    c_tab[0].wait()
    inner = [0, 1, 2, 3]
    transform(gather(vv, 0, inner) + gather(fv[0], 1, inner), [(ua, ud, inner), (fa, fd, inner)])

    h_f1 = send_row(fv[1], c_f1, 3)
    h_vel = send_row(wv, c_vel, 2)
    transform(gather(fv[1], 3, inner), [(fa1, fd1, inner)])
    def wide(value):
        return jnp.concatenate([value] * 4, axis=1)

    c_ir.wait()
    for n in range(25):
        irb[n] = jnp.broadcast_to(irv[:, n : n + 1], (8, LANES))
    c_sh.wait()
    c_im.wait()
    lane33 = lax.broadcasted_iota(jnp.int32, (8, 33), 1)
    sub33 = lax.broadcasted_iota(jnp.int32, (8, 33), 0)
    def mass(i):
        row = imv[i : i + 1, :] if i < 4 else imn[0:1, :]
        spread = jnp.broadcast_to(row, (8, 33))
        for j in range(4 if i < 4 else 5):
            picked = jnp.where(lane33 == 4 * sub33 + j, spread, 0.0)
            imb[5 * i + j] = jnp.broadcast_to(jnp.sum(picked, axis=1, keepdims=True), (8, LANES))
        if i < 4:
            imb[5 * i + 4] = jnp.broadcast_to(spread[:, 32:33], (8, LANES))
    for i in range(4):
        mass(i)
    for k in range(5):
        cb[k] = sum(float(DQ[i, k] * DQ[i, 2]) * sh[5 * i + 2] for i in (0, 1, 3, 4))
        cb[5 + k] = sum(float(DQ[i, k] * DQ[i, 2]) * sh[10 + i] for i in (0, 1, 3, 4))
    cross[0] = (DTIME * DTIME) * wide(imb[12]) * mask[0]
    cross[1] = cb[4]
    cross[2] = mask[0]
    h_cross = Link(cross, crossn, 5, True, (hs, hr))

    h_adj.wait()
    h_f0.wait()
    transform(gather(vv, 0, [4]) + gather(fv[0], 1, [4]), [(ua, ud, [4]), (fa, fd, [4])])

    def contraction(first, fa, fd, offs):
        def chunk(c, carry):
            ls = pl.ds(pl.multiple_of(c * LANES, LANES), LANES)
            for j in range(5) if 0 in offs else ():
                ns = [5 * k + j for k in range(5)]
                pa = apply5(DQ, [ua[n, :, ls] for n in ns])
                pf = apply5(DQ, [fa[n, :, ls] for n in ns])
                s = [sh[n, :, ls] * p for n, p in zip(ns, pa)]
                back = apply5(DQT, s)
                for k, n in enumerate(ns):
                    q[n, :, ls] = back[k]
                    term = pa[k] * pf[k]
                    kern[n, :, ls] = term if first else kern[n, :, ls] + term
            for i in offs:
                ns = [5 * i + k for k in range(5)]
                pa = apply5(DQ, [ua[n, :, ls] for n in ns])
                pf = apply5(DQ, [fa[n, :, ls] for n in ns])
                shs = [sh[n, :, ls] for n in ns]
                back = apply5(DQT, [a * b for a, b in zip(shs, pa)])
                for k, n in enumerate(ns):
                    q[n, :, ls] += back[k]
                    ir = irb[n]
                    p3 = ir * ud[n, :, ls]
                    kern[n, :, ls] += pa[k] * pf[k] + p3 * (ir * fd[n, :, ls])
                    z[n, :, ls] = ir * shs[k] * p3
            return carry

        lax.fori_loop(0, CHUNKS, chunk, 0)

    contraction(True, fa, fd, (0, 4))

    c_tab[1].wait()

    def back_rows(step, offs):
        rows_q = [q[5 * i : 5 * i + 5].reshape(40, WIDTH) for i in offs]
        rows_z = [z[5 * i : 5 * i + 5].reshape(40, WIDTH) for i in offs]
        (total,) = times(jnp.concatenate(rows_q, axis=0), (tab[4], tab[6]))
        (azimuthal,) = times(jnp.concatenate(rows_z, axis=0), (tab[5], tab[7]))
        total = total + azimuthal
        m = mask[0]
        for at, i in enumerate(offs):
            cc[step, 5 * i : 5 * i + 5] = total[40 * at : 40 * at + 40].reshape(5, 8, WIDTH) * m[None]

    def image(step, i):
        parts = [cc[step, 5 * i + j] for j in range(5)]
        if i == 0:
            parts = [a + cprev[step, j] for j, a in enumerate(parts)]
        return parts

    def update(step, i):
        parts = image(step, i)
        turned = pltpu.roll(parts[4], 1, 0)
        cols = [parts[0] + jnp.where(sub == 0, 0.0, turned), parts[1], parts[2], parts[3]]
        for j in range(4):
            gain = DTIME * wide(imb[5 * i + j])
            step_w = gain * cols[j]
            for c in range(4):
                new_w = wv[c][at(i, j), :] - step_w[:, LANES * c : LANES * (c + 1)]
                wv[c][at(i, j), :] = new_w
                vv[c][at(i, j), :] += DTIME * new_w
        last = turned[0:1]
        for c in range(4):
            row = slice(128 + i, 129 + i)
            gain = DTIME * imb[5 * i + 4][0:1]
            new_w = wv[c][row, :] - gain * last[:, LANES * c : LANES * (c + 1)]
            wv[c][row, :] = new_w
            vv[c][row, :] += DTIME * new_w

    def update_halo():
        parts = [cc[0, 20 + j] + cnext[j] for j in range(5)]
        left = pltpu.roll(parts[4], 1, 0)
        right = pltpu.roll(parts[0], 7, 0)
        cols = [parts[0] + jnp.where(sub == 0, 0.0, left), parts[1], parts[2], parts[3]]
        cols.append(parts[4] + jnp.where(sub == 7, 0.0, right))
        for j in range(5):
            halo[0, j] += DTIME * (halo[2, j] - DTIME * wide(imb[20 + j]) * cols[j])

    def ends(step):
        up = Link(cc.at[step, pl.ds(20, 5)], cprev.at[step], 2 * step, True, (cs, cr))
        return up, Link(cc.at[step, pl.ds(0, 5)], cnext, 1, False, (cs, cr)) if step == 0 else None

    back_rows(0, [4, 0])
    up0, down0 = ends(0)
    own = my * 4 + mx
    c_rf.wait()
    for copy in z_copies:
        copy.wait()
    for copy in id_copies:
        copy.wait()
    pl.semaphore_wait(relay, len(xpeer))
    ids = zid[0]
    for k in range(1, NZ):
        ids = ids + zid[k]
    ebuf[own] = ids
    pe = [remote(ebuf.at[own], ebuf.at[own], es.at[k], er.at[k], ppeer[k]) for k in range(15)]
    for c in range(4):
        g0[own, c] = zraw[:, 0, LANES * c : LANES * (c + 1)]
    p0 = [remote(g0.at[own], g0.at[own], g0s.at[k], g0r.at[k], ppeer[k]) for k in range(15)]
    for c in range(4):
        g1[own, c] = zraw[:, 1, LANES * c : LANES * (c + 1)]
    p1 = [remote(g1.at[own], g1.at[own], g1s.at[k], g1r.at[k], ppeer[k]) for k in range(15)]

    contraction(True, fa, fd, (1, 2, 3))
    back_rows(0, [1, 2, 3])

    for i in (1, 2, 3):
        update(0, i)
    transform(gather(vv, 0, [1, 2, 3]), [(ua, ud, [1, 2, 3])])
    h_im.wait()
    mass(4)
    h_vel.wait()
    h_f1.wait()
    up0.wait()
    down0.wait()
    update(0, 0)
    update_halo()
    transform(gather(vv, 0, [0, 4]) + gather(fv[1], 3, [4]), [(ua, ud, [0, 4]), (fa1, fd1, [4])])

    contraction(False, fa1, fd1, (0, 4))
    back_rows(1, [4, 0])
    up1, _ = ends(1)
    contraction(False, fa1, fd1, (1, 2, 3))
    back_rows(1, [1, 2, 3])
    for i in (1, 2, 3):
        update(1, i)
    for copy in pe:
        copy.wait()
    half = NY * NX
    r_lane = lax.broadcasted_iota(jnp.int32, (half, 8, LANES), 2)
    r_sub = lax.broadcasted_iota(jnp.int32, (half, 8, LANES), 1)
    group = r_lane // 16 == r_sub
    ids_all = jnp.broadcast_to(ebuf[...], (half, 8, LANES))

    def onehot(dev):
        target = ((dev - 1) * 8 + r_lane % 16).astype(F32)
        hit = (ids_all == target) & group
        return jnp.where(hit, 1.0, 0.0).reshape(half * 8, LANES).T.astype(BF16)

    pick = jnp.concatenate([onehot(core), onehot(me)], axis=0)

    for copy in p0:
        copy.wait()

    def sums(g, k):
        for c in range(4):
            high, low = split(g[:, c].reshape(half * 8, LANES))
            total = dot(pick, high) + dot(pick, low)
            for d, ref in ((0, psend), (LANES, pown)):
                acc = total[d : d + 16]
                for t in range(1, 8):
                    acc = acc + total[d + 16 * t : d + 16 * t + 16]
                ref[k, :, LANES * c : LANES * (c + 1)] = acc
        return remote(psend.at[k], precv.at[k], ps.at[k], pr.at[k], core)

    k0 = sums(g0, 0)
    for copy in p1:
        copy.wait()
    k1 = sums(g1, 1)
    h_cross.wait()

    turn = wide(irb[12])
    col_f = apply5(DQ, [fa1[5 * k + 2] for k in range(5)])
    row_f = apply5(DQ, [fa1[10 + k] for k in range(5)])
    k0.wait()
    source0 = pown[0] + precv[0]
    kick = DTIME * wide(imb[12]) * source0[8:16]
    moved = jnp.concatenate([kick * (DTIME * mask[0]), crossn[0] * source0[0:8]], axis=0)
    plain, deriv = times(moved, (tab[0], tab[2]), (tab[1], tab[3]))
    before, plain, deriv = plain[8:16], plain[0:8], deriv[0:8]
    for k in (0, 1, 3, 4):
        kern[5 * k + 2] += float(DQ[k, 2]) * plain * col_f[k]
        kern[10 + k] += float(DQ[k, 2]) * plain * row_f[k]
    kern[12] += (turn * deriv) * (turn * fd1[12])
    terms = [cb[k] * plain for k in (0, 1, 3)] + [cb[5 + k] * plain for k in (0, 1, 3, 4)]
    terms += [crossn[1] * before, (cb[2] + cb[7]) * plain]
    (back,) = times(jnp.concatenate(terms, axis=0), (tab[4], tab[6]))
    (extra,) = times(turn * turn * sh[12] * deriv, (tab[5], tab[7]))
    b = [back[8 * k : 8 * k + 8] * mask[0] for k in range(7)]
    before = back[56:64] * crossn[2]
    middle = (back[64:72] + extra) * mask[0]
    turned = pltpu.roll(b[6], 1, 0)
    fix = {(0, 2): b[0] + before, (1, 2): b[1], (3, 2): b[2]}
    fix[(2, 0)] = b[3] + jnp.where(sub == 0, 0.0, turned)
    fix[(2, 1)], fix[(2, 3)], fix[(2, 2)] = b[4], b[5], middle
    k1.wait()
    kick1 = DTIME * wide(imb[12]) * (pown[1, 8:16] + precv[1, 8:16])
    up1.wait()
    update(1, 0)
    for (i, j), value in fix.items():
        move = -(DTIME * wide(imb[5 * i + j])) * value
        shift = DTIME * move
        if (i, j) == (2, 2):
            move = move + kick + kick1
            shift = DTIME * (move + kick)
        for c in range(4):
            ls = slice(LANES * c, LANES * (c + 1))
            wv[c][at(i, j), :] += move[:, ls]
            vv[c][at(i, j), :] += shift[:, ls]
    for c in range(4):
        move = -(DTIME * imb[14][0:1]) * turned[0:1, LANES * c : LANES * (c + 1)]
        wv[c][130:131, :] += move
        vv[c][130:131, :] += DTIME * move
    outs = []
    for c in range(4):
        ls = pl.ds(LANES * c, LANES)
        copy = pltpu.make_async_copy(v.at[c], out_v.at[:, :, ls], osem.at[c])
        copy.start()
        outs.append(copy)
        copy = pltpu.make_async_copy(w.at[c], out_w.at[:, :, ls], osem.at[4 + c])
        copy.start()
        outs.append(copy)
    for copy in outs:
        copy.wait()


def finish(a, b, c, oa, ob, oc, sem):
    copies = [pltpu.make_async_copy(x, y, sem.at[k]) for k, (x, y) in enumerate([(a, oa), (b, ob), (c, oc)])]
    for copy in copies:
        copy.start()
    for copy in copies:
        copy.wait()


def per_device(adj, vel, fwd, shear, inv_rad, inv_mass, counts, rec_elem, rec_force):
    table = jnp.asarray(tables())
    node = (4, 33, 4, LANES)
    elem = (25, 8, WIDTH)
    dma = pltpu.SemaphoreType.DMA
    scratch = [
        pltpu.VMEM(node, F32),
        pltpu.VMEM(node, F32),
        pltpu.VMEM((2,) + node, F32),
        pltpu.VMEM((8, WIDTH, WIDTH), BF16),
        pltpu.VMEM(elem, F32),
        pltpu.VMEM((8, 25), F32),
        pltpu.VMEM((25, 8, LANES), F32),
        pltpu.VMEM((4, 33), F32),
        pltpu.VMEM((4, 33), F32),
        pltpu.VMEM((25, 8, LANES), F32),
        pltpu.SMEM((8,), jnp.int32),
        pltpu.SMEM((1,), jnp.int32),
        pltpu.VMEM(elem, F32),
        pltpu.VMEM(elem, F32),
        pltpu.VMEM(elem, F32),
        pltpu.VMEM(elem, F32),
        pltpu.VMEM(elem, F32),
        pltpu.VMEM(elem, F32),
        pltpu.VMEM(elem, F32),
        pltpu.VMEM(elem, F32),
        pltpu.VMEM((2,) + elem, F32),
        pltpu.VMEM((2, 5, 8, WIDTH), F32),
        pltpu.VMEM((5, 8, WIDTH), F32),
        pltpu.VMEM((2, 8, WIDTH), F32),
        pltpu.VMEM((4, 5, 8, WIDTH), F32),
        pltpu.VMEM((4, 5, 8, WIDTH), F32),
        pltpu.VMEM((3, 8, WIDTH), F32),
        pltpu.VMEM((3, 8, WIDTH), F32),
        pltpu.VMEM((10, 8, WIDTH), F32),
        pltpu.VMEM((NZ, 2, WIDTH), F32),
        pltpu.VMEM((NZ, 1, LANES), F32),
        pltpu.VMEM((NY * NX, 4, 8, LANES), F32),
        pltpu.VMEM((NY * NX, 4, 8, LANES), F32),
        pltpu.VMEM((NY * NX, 1, LANES), F32),
        pltpu.VMEM((2, 16, WIDTH), F32),
        pltpu.VMEM((2, 16, WIDTH), F32),
        pltpu.VMEM((2, 16, WIDTH), F32),
        dma((22,)),
        dma((2,)),
        dma((8,)),
        dma((6,)),
        dma((6,)),
        dma((7,)),
        dma((7,)),
        dma((7,)),
        dma((7,)),
        dma((15,)),
        dma((15,)),
        dma((15,)),
        dma((15,)),
        dma((15,)),
        dma((15,)),
        dma((4,)),
        dma((4,)),
        dma((2,)),
        dma((2,)),
        pltpu.SemaphoreType.REGULAR,
    ]
    shapes = [
        jax.ShapeDtypeStruct((33, 4, WIDTH), F32),
        jax.ShapeDtypeStruct((33, 4, WIDTH), F32),
        jax.ShapeDtypeStruct((25, 8, WIDTH), F32),
    ]
    new_disp, new_vel, kernel = pl.pallas_call(
        body,
        out_shape=[pltpu.VMEM(t.shape, F32) for t in shapes],
        in_specs=[pl.BlockSpec(memory_space=pltpu.HBM)] * 10,
        out_specs=[pl.BlockSpec(memory_space=pltpu.VMEM)] * 3,
        scratch_shapes=scratch,
        compiler_params=pltpu.CompilerParams(
            collective_id=0, has_side_effects=True, vmem_limit_bytes=62 * 2**20
        ),
        name="adjoint_steps",
    )(
        jnp.transpose(adj, (1, 0, 2)),
        jnp.transpose(vel, (1, 0, 2)),
        jnp.transpose(fwd, (0, 2, 1, 3)),
        jnp.transpose(shear, (1, 0, 2)),
        inv_rad,
        inv_mass,
        counts,
        rec_elem,
        rec_force,
        table,
    )
    outs = pl.pallas_call(
        finish,
        out_shape=shapes,
        in_specs=[pl.BlockSpec(memory_space=pltpu.VMEM)] * 3,
        out_specs=[pl.BlockSpec(memory_space=pltpu.HBM)] * 3,
        scratch_shapes=[dma((3,))],
        name="results",
    )(*(pltpu.with_memory_space_constraint(x, pltpu.VMEM) for x in (new_disp, new_vel, kernel)))
    return tuple(jnp.transpose(out, (1, 0, 2)) for out in outs)


def solution(mesh):
    in_specs = (
        P("dom", None, None),
        P("dom", None, None),
        P(None, "dom", None, None),
        P("dom", None, None),
        P("dom", None),
        P("dom", None),
        P("dom"),
        P("dom"),
        P("dom", None, None),
    )
    out_specs = (P("dom", None, None), P("dom", None, None), P("dom", None, None))
    return jax.shard_map(per_device, mesh=mesh, in_specs=in_specs, out_specs=out_specs, check_vma=False)
```

```python
import functools

import jax
import jax.numpy as jnp
import ml_dtypes
import numpy as np
from jax import lax
from jax.experimental import pallas as pl
from jax.experimental.pallas import tpu as pltpu
from jax.sharding import PartitionSpec as P

GSCALE = 0.25
DTIME = 0.25
NZ, NY, NX, NCORE = 8, 4, 4, 2
NDEV = NZ * NY * NX * NCORE
LANES = 128
CHUNKS = 4
MODES = 256
WIDTH = 512
MESH = pl.DeviceIdType.MESH
F32 = jnp.float32
BF16 = jnp.bfloat16


def gll_derivative():
    points = np.array([-1.0, -np.sqrt(3.0 / 7.0), 0.0, np.sqrt(3.0 / 7.0), 1.0])
    legendre = (35.0 * points**4 - 30.0 * points**2 + 3.0) / 8.0
    matrix = np.zeros((5, 5))
    for row in range(5):
        for col in range(5):
            if row != col:
                matrix[row, col] = legendre[row] / (legendre[col] * (points[row] - points[col]))
    matrix[0, 0] = -5.0
    matrix[4, 4] = 5.0
    return matrix


DQ = GSCALE * gll_derivative()
DQT = DQ.T


def tables():
    mode = np.arange(MODES)[:, None]
    angle = 2.0 * np.pi * (mode * np.arange(WIDTH)[None, :] % WIDTH) / WIDTH
    scale = 1.0 / np.sqrt(MODES)
    cos, sin = np.cos(angle) * scale, np.sin(angle) * scale
    plain = np.concatenate([cos, -sin], axis=0)
    deriv = np.concatenate([-mode * sin, -mode * cos], axis=0)

    def parts(table):
        high = table.astype(ml_dtypes.bfloat16)
        low = (table - high.astype(np.float64)).astype(ml_dtypes.bfloat16)
        return high, low

    ph, plo = parts(plain)
    dh, dlo = parts(deriv)
    return np.stack([ph, dh, plo, dlo, ph.T, dh.T, plo.T, dlo.T])


def apply5(mat, x):
    even = [x[0] + x[4], x[1] + x[3]]
    odd = [x[0] - x[4], x[1] - x[3]]

    def combine(terms):
        total = None
        for coef, value in terms:
            if abs(coef) > 1e-12:
                term = float(coef) * value
                total = term if total is None else total + term
        return total

    out = [None] * 5
    for i in range(2):
        s = combine([(0.5 * (mat[i, k] - mat[i, 4 - k]), odd[k]) for k in range(2)])
        d = combine([(0.5 * (mat[i, k] + mat[i, 4 - k]), even[k]) for k in range(2)] + [(mat[i, 2], x[2])])
        out[i] = s + d
        out[4 - i] = s - d
    out[2] = combine([(mat[2, k], odd[k]) for k in range(2)])
    return out


def split(value):
    high = value.astype(BF16)
    return high, (value - high.astype(F32)).astype(BF16)


def dot(a, b):
    return lax.dot_general(a, b, (((1,), (0,)), ((), ())), preferred_element_type=F32)


def times(x, *parts):
    rows = x.shape[0]
    high = x.astype(BF16)
    both = jnp.concatenate([x, x - high.astype(F32)], axis=0).astype(BF16)
    out = []
    for table_high, table_low in parts:
        first = dot(both, table_high)
        out.append(first[:rows] + first[rows:] + dot(high, table_low))
    return out


def body(
    adj, vel, fwd, shear, inv_rad, inv_mass, counts, rec_elem, rec_force, table,
    v, w, kern,
    f, tab, sh, irv, irb, imv, imn, imb, cnt, rel,
    ua, ud, fa, fd, fa1, fd1, q, z, cc, cprev, cnext, mask, halo, edge,
    cross, crossn, cb, zraw, zid, g0, psend, precv, pown,
    lsem, tsem, hs, hr, zs, zr, zis, zir, g0s, g0r, cs, cr, ps, pr, relay,
):
    me = lax.axis_index("dom")
    mz, my, mx, mc = me // 32, (me // 8) % 4, (me // 2) % 4, me % 2
    nxt = (me + 1) % NDEV
    prv = (me + NDEV - 1) % NDEV
    zpeer = [((mz + k) % NZ) * 32 + me % 32 for k in range(1, NZ)]
    shifts = [(0, 2), (2, 0), (2, 2), (1, 2), (2, 1), (3, 2), (2, 3), (1, 1), (1, 3), (3, 1), (3, 3), (0, 1), (1, 0), (0, 3), (3, 0)]
    ppeer = [mz * 32 + ((my + j) % NY) * 8 + ((mx + k) % NX) * 2 + mc for j, k in shifts]
    xpeer = [me - mx * 2 + ((mx + k) % NX) * 2 for k in range(1, NX)]
    ypeer = [me - my * 8 + ((my + k) % NY) * 8 for k in range(1, NY)]
    core = me + 1 - 2 * mc

    barrier = pltpu.get_barrier_semaphore()
    peers = zpeer + xpeer + ypeer + [core]
    for peer in peers:
        pl.semaphore_signal(barrier, inc=1, device_id=(peer,), device_id_type=MESH)
    above, below = me < NDEV - 1, me > 0

    @pl.when(above)
    def _():
        pl.semaphore_signal(barrier, inc=1, device_id=(nxt,), device_id_type=MESH)

    @pl.when(below)
    def _():
        pl.semaphore_signal(barrier, inc=1, device_id=(prv,), device_id_type=MESH)

    def local(src, dst, k):
        copy = pltpu.make_async_copy(src, dst, lsem.at[k])
        copy.start()
        return copy

    c_rf = local(rec_force.at[0], zraw.at[mz], 0)
    c_rel = local(rec_elem, rel, 1)
    c_cnt = local(counts, cnt, 2)
    c_adj = [local(adj.at[:, :, pl.ds(LANES * c, LANES)], v.at[c], 3 + c) for c in range(4)]
    c_tab = [
        pltpu.make_async_copy(table.at[pl.ds(4 * k, 4)], tab.at[pl.ds(4 * k, 4)], tsem.at[k]) for k in range(2)
    ]
    c_tab[0].start()
    c_f0 = [local(fwd.at[0, :, :, pl.ds(LANES * c, LANES)], f.at[0, c], 7 + c) for c in range(4)]
    c_ir = local(inv_rad, irv, 11)
    c_im = local(inv_mass, imv, 12)
    c_sh = local(shear, sh, 13)
    c_vel = [local(vel.at[:, :, pl.ds(LANES * c, LANES)], w.at[c], 14 + c) for c in range(4)]
    c_f1 = [local(fwd.at[1, :, :, pl.ds(LANES * c, LANES)], f.at[1, c], 18 + c) for c in range(4)]

    vv = [v.at[c].reshape(132, LANES) for c in range(4)]
    wv = [w.at[c].reshape(132, LANES) for c in range(4)]
    fv = [[f.at[s, c].reshape(132, LANES) for c in range(4)] for s in range(2)]

    def at(i, j):
        return pl.ds(4 * j + i, 8, stride=16)

    lane = lax.broadcasted_iota(jnp.int32, (8, WIDTH), 1)
    sub = lax.broadcasted_iota(jnp.int32, (8, WIDTH), 0)
    missing = (me + NDEV - 1) // NDEV - me // (NDEV - 1)
    pl.semaphore_wait(barrier, len(peers) + 1 + missing)

    def remote(src, dst, ssem, rsem, dev):
        copy = pltpu.make_async_remote_copy(
            src_ref=src, dst_ref=dst, send_sem=ssem, recv_sem=rsem, device_id=(dev,), device_id_type=MESH
        )
        copy.start()
        return copy

    class Link:
        def __init__(self, src, dst, k, up, sems):
            self.sends, self.takes = (above, below) if up else (below, above)
            self.copy = pltpu.make_async_remote_copy(
                src_ref=src,
                dst_ref=dst,
                send_sem=sems[0].at[k],
                recv_sem=sems[1].at[k],
                device_id=(nxt if up else prv,),
                device_id_type=MESH,
            )

            @pl.when(self.sends)
            def _():
                self.copy.start()

        def wait(self):
            @pl.when(self.takes)
            def _():
                self.copy.wait_recv()

            @pl.when(self.sends)
            def _():
                self.copy.wait_send()

    z_copies = [remote(rec_force.at[0], zraw.at[mz], zs.at[k], zr.at[k], zpeer[k]) for k in range(NZ - 1)]
    c_rel.wait()
    own_id = jnp.full((1, LANES), rel[0], jnp.int32).astype(F32)
    zid[mz] = own_id
    id_copies = [remote(zid.at[mz], zid.at[mz], zis.at[k], zir.at[k], zpeer[k]) for k in range(NZ - 1)]

    def send_row(view, copies, k):
        for copy in copies:
            copy.wait()
        for j in range(5):
            for c in range(4):
                edge[k, j, :, LANES * c : LANES * (c + 1)] = view[c][at(0, j), :]
        return Link(edge.at[k], halo.at[k], k, False, (hs, hr))

    h_adj = send_row(vv, c_adj, 0)
    h_f0 = send_row(fv[0], c_f0, 1)
    h_im = Link(inv_mass, imn, 4, False, (hs, hr))

    for peer in xpeer:
        pl.semaphore_signal(relay, inc=1, device_id=(peer,), device_id_type=MESH)

    c_cnt.wait()
    limit = jnp.zeros((8, WIDTH), jnp.int32)
    for e in range(8):
        limit = jnp.where(sub == e, cnt[e], limit)
    live = (lane % MODES < limit).astype(F32)
    mask[0] = live
    mask[1] = live * jnp.where(me == NDEV - 1, 0.0, 1.0)

    @pl.when(me == NDEV - 1)
    def _():
        halo[...] = jnp.zeros(halo.shape, F32)
        cnext[...] = jnp.zeros(cnext.shape, F32)
        imn[...] = jnp.zeros(imn.shape, F32)

    @pl.when(me == 0)
    def _():
        cprev[...] = jnp.zeros(cprev.shape, F32)
        crossn[...] = jnp.zeros(crossn.shape, F32)


    def rows(view, k, i):
        out = []
        for j in range(5):
            if i == 4:
                out.append(halo[k, j] * mask[1])
            else:
                out.append(jnp.concatenate([view[c][at(i, j), :] for c in range(4)], axis=1) * mask[0])
        return out

    def transform(pieces, dests):
        plain, deriv = times(jnp.concatenate(pieces, axis=0), (tab[0], tab[2]), (tab[1], tab[3]))
        at = 0
        for dst, dst_d, offs in dests:
            for i in offs:
                dst[5 * i : 5 * i + 5] = plain[at : at + 40].reshape(5, 8, WIDTH)
                dst_d[5 * i : 5 * i + 5] = deriv[at : at + 40].reshape(5, 8, WIDTH)
                at += 40

    def gather(view, k, offs):
        out = []
        for i in offs:
            out += rows(view, k, i)
        return out

    c_tab[0].wait()
    inner = [0, 1, 2, 3]
    transform(gather(vv, 0, inner) + gather(fv[0], 1, inner), [(ua, ud, inner), (fa, fd, inner)])

    c_tab[1].start()
    h_f1 = send_row(fv[1], c_f1, 3)
    h_vel = send_row(wv, c_vel, 2)
    transform(gather(fv[1], 3, inner), [(fa1, fd1, inner)])
    def wide(value):
        return jnp.concatenate([value] * 4, axis=1)

    c_ir.wait()
    for n in range(25):
        irb[n] = jnp.broadcast_to(irv[:, n : n + 1], (8, LANES))
    c_sh.wait()
    c_im.wait()
    lane33 = lax.broadcasted_iota(jnp.int32, (8, 33), 1)
    sub33 = lax.broadcasted_iota(jnp.int32, (8, 33), 0)
    def mass(i):
        row = imv[i : i + 1, :] if i < 4 else imn[0:1, :]
        spread = jnp.broadcast_to(row, (8, 33))
        for j in range(4 if i < 4 else 5):
            picked = jnp.where(lane33 == 4 * sub33 + j, spread, 0.0)
            imb[5 * i + j] = jnp.broadcast_to(jnp.sum(picked, axis=1, keepdims=True), (8, LANES))
        if i < 4:
            imb[5 * i + 4] = jnp.broadcast_to(spread[:, 32:33], (8, LANES))
    for i in range(4):
        mass(i)
    for k in range(5):
        cb[k] = sum(float(DQ[i, k] * DQ[i, 2]) * sh[5 * i + 2] for i in (0, 1, 3, 4))
        cb[5 + k] = sum(float(DQ[i, k] * DQ[i, 2]) * sh[10 + i] for i in (0, 1, 3, 4))
    cross[0] = (DTIME * DTIME) * wide(imb[12]) * mask[0]
    cross[1] = cb[4]
    cross[2] = mask[0]
    h_cross = Link(cross, crossn, 5, True, (hs, hr))

    h_adj.wait()
    h_f0.wait()
    transform(gather(vv, 0, [4]) + gather(fv[0], 1, [4]), [(ua, ud, [4]), (fa, fd, [4])])

    def contraction(first, fa, fd, offs):
        def chunk(c, carry):
            ls = pl.ds(pl.multiple_of(c * LANES, LANES), LANES)
            for j in range(5) if 0 in offs else ():
                ns = [5 * k + j for k in range(5)]
                pa = apply5(DQ, [ua[n, :, ls] for n in ns])
                pf = apply5(DQ, [fa[n, :, ls] for n in ns])
                s = [sh[n, :, ls] * p for n, p in zip(ns, pa)]
                back = apply5(DQT, s)
                for k, n in enumerate(ns):
                    q[n, :, ls] = back[k]
                    term = pa[k] * pf[k]
                    kern[n, :, ls] = term if first else kern[n, :, ls] + term
            for i in offs:
                ns = [5 * i + k for k in range(5)]
                pa = apply5(DQ, [ua[n, :, ls] for n in ns])
                pf = apply5(DQ, [fa[n, :, ls] for n in ns])
                shs = [sh[n, :, ls] for n in ns]
                back = apply5(DQT, [a * b for a, b in zip(shs, pa)])
                for k, n in enumerate(ns):
                    q[n, :, ls] += back[k]
                    ir = irb[n]
                    p3 = ir * ud[n, :, ls]
                    kern[n, :, ls] += pa[k] * pf[k] + p3 * (ir * fd[n, :, ls])
                    z[n, :, ls] = ir * shs[k] * p3
            return carry

        lax.fori_loop(0, CHUNKS, chunk, 0, unroll=True)

    contraction(True, fa, fd, (0, 4))

    c_tab[1].wait()

    def back_rows(step, offs):
        rows_q = [q[5 * i : 5 * i + 5].reshape(40, WIDTH) for i in offs]
        rows_z = [z[5 * i : 5 * i + 5].reshape(40, WIDTH) for i in offs]
        (total,) = times(jnp.concatenate(rows_q, axis=0), (tab[4], tab[6]))
        (azimuthal,) = times(jnp.concatenate(rows_z, axis=0), (tab[5], tab[7]))
        total = total + azimuthal
        m = mask[0]
        for at, i in enumerate(offs):
            cc[step, 5 * i : 5 * i + 5] = total[40 * at : 40 * at + 40].reshape(5, 8, WIDTH) * m[None]

    def image(step, i):
        parts = [cc[step, 5 * i + j] for j in range(5)]
        if i == 0:
            parts = [a + cprev[step, j] for j, a in enumerate(parts)]
        return parts

    def update(step, i):
        parts = image(step, i)
        turned = pltpu.roll(parts[4], 1, 0)
        cols = [parts[0] + jnp.where(sub == 0, 0.0, turned), parts[1], parts[2], parts[3]]
        for j in range(4):
            gain = DTIME * wide(imb[5 * i + j])
            step_w = gain * cols[j]
            for c in range(4):
                new_w = wv[c][at(i, j), :] - step_w[:, LANES * c : LANES * (c + 1)]
                wv[c][at(i, j), :] = new_w
                vv[c][at(i, j), :] += DTIME * new_w
        last = turned[0:1]
        for c in range(4):
            row = slice(128 + i, 129 + i)
            gain = DTIME * imb[5 * i + 4][0:1]
            new_w = wv[c][row, :] - gain * last[:, LANES * c : LANES * (c + 1)]
            wv[c][row, :] = new_w
            vv[c][row, :] += DTIME * new_w

    def update_halo():
        parts = [cc[0, 20 + j] + cnext[j] for j in range(5)]
        left = pltpu.roll(parts[4], 1, 0)
        right = pltpu.roll(parts[0], 7, 0)
        cols = [parts[0] + jnp.where(sub == 0, 0.0, left), parts[1], parts[2], parts[3]]
        cols.append(parts[4] + jnp.where(sub == 7, 0.0, right))
        for j in range(5):
            halo[0, j] += DTIME * (halo[2, j] - DTIME * wide(imb[20 + j]) * cols[j])

    def ends(step):
        up = Link(cc.at[step, pl.ds(20, 5)], cprev.at[step], 2 * step, True, (cs, cr))
        return up, Link(cc.at[step, pl.ds(0, 5)], cnext, 1, False, (cs, cr)) if step == 0 else None

    back_rows(0, [4, 0])
    up0, down0 = ends(0)
    own = my * 4 + mx
    c_rf.wait()
    for copy in z_copies:
        copy.wait()
    for copy in id_copies:
        copy.wait()
    pl.semaphore_wait(relay, len(xpeer))
    for k in range(NZ):
        g0[own, 4, k : k + 1, :] = zid[k]
    for c in range(4):
        g0[own, c] = zraw[:, 0, LANES * c : LANES * (c + 1)]
        g0[own, 5 + c] = zraw[:, 1, LANES * c : LANES * (c + 1)]
    p0 = [remote(g0.at[own], g0.at[own], g0s.at[k], g0r.at[k], ppeer[k]) for k in range(15)]

    contraction(True, fa, fd, (1, 2, 3))
    back_rows(0, [1, 2, 3])

    for i in (1, 2, 3):
        update(0, i)
    transform(gather(vv, 0, [1, 2, 3]), [(ua, ud, [1, 2, 3])])
    h_im.wait()
    mass(4)
    h_vel.wait()
    h_f1.wait()
    up0.wait()
    down0.wait()
    update(0, 0)
    update_halo()
    transform(gather(vv, 0, [0, 4]) + gather(fv[1], 3, [4]), [(ua, ud, [0, 4]), (fa1, fd1, [4])])

    contraction(False, fa1, fd1, (0, 4))
    back_rows(1, [4, 0])
    up1, _ = ends(1)
    contraction(False, fa1, fd1, (1, 2, 3))
    back_rows(1, [1, 2, 3])
    for i in (1, 2, 3):
        update(1, i)
    for copy in p0:
        copy.wait()
    half = NY * NX
    r_lane = lax.broadcasted_iota(jnp.int32, (half, 8, LANES), 2)
    r_sub = lax.broadcasted_iota(jnp.int32, (half, 8, LANES), 1)
    group = r_lane // 16 == r_sub
    ids_all = g0[:, 4]

    def onehot(dev):
        target = ((dev - 1) * 8 + r_lane % 16).astype(F32)
        hit = (ids_all == target) & group
        return jnp.where(hit, 1.0, 0.0).reshape(half * 8, LANES).T.astype(BF16)

    pick = jnp.concatenate([onehot(core), onehot(me)], axis=0)

    def sums(first, k):
        for c in range(4):
            high, low = split(g0[:, first + c].reshape(half * 8, LANES))
            total = dot(pick, high) + dot(pick, low)
            for d, ref in ((0, psend), (LANES, pown)):
                acc = total[d : d + 16]
                for t in range(1, 8):
                    acc = acc + total[d + 16 * t : d + 16 * t + 16]
                ref[k, :, LANES * c : LANES * (c + 1)] = acc
        return remote(psend.at[k], precv.at[k], ps.at[k], pr.at[k], core)

    k0 = sums(0, 0)
    k1 = sums(5, 1)
    h_cross.wait()

    turn = wide(irb[12])
    col_f = apply5(DQ, [fa1[5 * k + 2] for k in range(5)])
    row_f = apply5(DQ, [fa1[10 + k] for k in range(5)])
    k0.wait()
    source0 = pown[0] + precv[0]
    kick = DTIME * wide(imb[12]) * source0[8:16]
    moved = jnp.concatenate([kick * (DTIME * mask[0]), crossn[0] * source0[0:8]], axis=0)
    plain, deriv = times(moved, (tab[0], tab[2]), (tab[1], tab[3]))
    before, plain, deriv = plain[8:16], plain[0:8], deriv[0:8]
    for k in (0, 1, 3, 4):
        kern[5 * k + 2] += float(DQ[k, 2]) * plain * col_f[k]
        kern[10 + k] += float(DQ[k, 2]) * plain * row_f[k]
    kern[12] += (turn * deriv) * (turn * fd1[12])
    terms = [cb[k] * plain for k in (0, 1, 3)] + [cb[5 + k] * plain for k in (0, 1, 3, 4)]
    terms += [crossn[1] * before, (cb[2] + cb[7]) * plain]
    (back,) = times(jnp.concatenate(terms, axis=0), (tab[4], tab[6]))
    (extra,) = times(turn * turn * sh[12] * deriv, (tab[5], tab[7]))
    b = [back[8 * k : 8 * k + 8] * mask[0] for k in range(7)]
    before = back[56:64] * crossn[2]
    middle = (back[64:72] + extra) * mask[0]
    turned = pltpu.roll(b[6], 1, 0)
    fix = {(0, 2): b[0] + before, (1, 2): b[1], (3, 2): b[2]}
    fix[(2, 0)] = b[3] + jnp.where(sub == 0, 0.0, turned)
    fix[(2, 1)], fix[(2, 3)], fix[(2, 2)] = b[4], b[5], middle
    k1.wait()
    kick1 = DTIME * wide(imb[12]) * (pown[1, 8:16] + precv[1, 8:16])
    up1.wait()
    update(1, 0)
    for (i, j), value in fix.items():
        move = -(DTIME * wide(imb[5 * i + j])) * value
        shift = DTIME * move
        if (i, j) == (2, 2):
            move = move + kick + kick1
            shift = DTIME * (move + kick)
        for c in range(4):
            ls = slice(LANES * c, LANES * (c + 1))
            wv[c][at(i, j), :] += move[:, ls]
            vv[c][at(i, j), :] += shift[:, ls]
    for c in range(4):
        move = -(DTIME * imb[14][0:1]) * turned[0:1, LANES * c : LANES * (c + 1)]
        wv[c][130:131, :] += move
        vv[c][130:131, :] += DTIME * move


def finish(a, b, c, oa, ob, oc, sem):
    copies = [pltpu.make_async_copy(c, oc, sem.at[8])]
    for k in range(4):
        ls = pl.ds(LANES * k, LANES)
        copies.append(pltpu.make_async_copy(a.at[k], oa.at[:, :, ls], sem.at[k]))
        copies.append(pltpu.make_async_copy(b.at[k], ob.at[:, :, ls], sem.at[4 + k]))
    for copy in copies:
        copy.start()
    for copy in copies:
        copy.wait()


def per_device(adj, vel, fwd, shear, inv_rad, inv_mass, counts, rec_elem, rec_force):
    table = jnp.asarray(tables())
    node = (4, 33, 4, LANES)
    elem = (25, 8, WIDTH)
    dma = pltpu.SemaphoreType.DMA
    scratch = [
        pltpu.VMEM((2,) + node, F32),
        pltpu.VMEM((8, WIDTH, WIDTH), BF16),
        pltpu.VMEM(elem, F32),
        pltpu.VMEM((8, 25), F32),
        pltpu.VMEM((25, 8, LANES), F32),
        pltpu.VMEM((4, 33), F32),
        pltpu.VMEM((4, 33), F32),
        pltpu.VMEM((25, 8, LANES), F32),
        pltpu.SMEM((8,), jnp.int32),
        pltpu.SMEM((1,), jnp.int32),
        pltpu.VMEM(elem, F32),
        pltpu.VMEM(elem, F32),
        pltpu.VMEM(elem, F32),
        pltpu.VMEM(elem, F32),
        pltpu.VMEM(elem, F32),
        pltpu.VMEM(elem, F32),
        pltpu.VMEM(elem, F32),
        pltpu.VMEM(elem, F32),
        pltpu.VMEM((2,) + elem, F32),
        pltpu.VMEM((2, 5, 8, WIDTH), F32),
        pltpu.VMEM((5, 8, WIDTH), F32),
        pltpu.VMEM((2, 8, WIDTH), F32),
        pltpu.VMEM((4, 5, 8, WIDTH), F32),
        pltpu.VMEM((4, 5, 8, WIDTH), F32),
        pltpu.VMEM((3, 8, WIDTH), F32),
        pltpu.VMEM((3, 8, WIDTH), F32),
        pltpu.VMEM((10, 8, WIDTH), F32),
        pltpu.VMEM((NZ, 2, WIDTH), F32),
        pltpu.VMEM((NZ, 1, LANES), F32),
        pltpu.VMEM((NY * NX, 9, 8, LANES), F32),
        pltpu.VMEM((2, 16, WIDTH), F32),
        pltpu.VMEM((2, 16, WIDTH), F32),
        pltpu.VMEM((2, 16, WIDTH), F32),
        dma((22,)),
        dma((2,)),
        dma((6,)),
        dma((6,)),
        dma((7,)),
        dma((7,)),
        dma((7,)),
        dma((7,)),
        dma((15,)),
        dma((15,)),
        dma((4,)),
        dma((4,)),
        dma((2,)),
        dma((2,)),
        pltpu.SemaphoreType.REGULAR,
    ]
    shapes = [
        jax.ShapeDtypeStruct((33, 4, WIDTH), F32),
        jax.ShapeDtypeStruct((33, 4, WIDTH), F32),
        jax.ShapeDtypeStruct((25, 8, WIDTH), F32),
    ]
    new_disp, new_vel, kernel = pl.pallas_call(
        body,
        out_shape=[pltpu.VMEM(shape, F32) for shape in (node, node, elem)],
        in_specs=[pl.BlockSpec(memory_space=pltpu.HBM)] * 10,
        out_specs=[pl.BlockSpec(memory_space=pltpu.VMEM)] * 3,
        scratch_shapes=scratch,
        compiler_params=pltpu.CompilerParams(
            collective_id=0, has_side_effects=True, vmem_limit_bytes=62 * 2**20
        ),
        name="adjoint_steps",
    )(
        jnp.transpose(adj, (1, 0, 2)),
        jnp.transpose(vel, (1, 0, 2)),
        jnp.transpose(fwd, (0, 2, 1, 3)),
        jnp.transpose(shear, (1, 0, 2)),
        inv_rad,
        inv_mass,
        counts,
        rec_elem,
        rec_force,
        table,
    )
    outs = pl.pallas_call(
        finish,
        out_shape=shapes,
        in_specs=[pl.BlockSpec(memory_space=pltpu.VMEM)] * 3,
        out_specs=[pl.BlockSpec(memory_space=pltpu.HBM)] * 3,
        scratch_shapes=[dma((9,))],
        name="results",
    )(*(pltpu.with_memory_space_constraint(x, pltpu.VMEM) for x in (new_disp, new_vel, kernel)))
    return tuple(jnp.transpose(out, (1, 0, 2)) for out in outs)


def solution(mesh):
    in_specs = (
        P("dom", None, None),
        P("dom", None, None),
        P(None, "dom", None, None),
        P("dom", None, None),
        P("dom", None),
        P("dom", None),
        P("dom"),
        P("dom"),
        P("dom", None, None),
    )
    out_specs = (P("dom", None, None), P("dom", None, None), P("dom", None, None))
    return jax.shard_map(per_device, mesh=mesh, in_specs=in_specs, out_specs=out_specs, check_vma=False)
```
